32 devices in a mesh: bulk: 4 (over x, core), valve: 8 (over z, y).
Axes of the slice: x: 2, y: 2, z: 4, core: 2. Of those that a mesh axis runs over, the one named last changes fastest.
Arguments:
- bg_adjoint: float32 [5, 32, 256, 128], P(None, 'bulk', 'valve'), may hold values from -6 to 6
- bg_velocity: float32 [3, 32, 256, 128], P(None, 'bulk', 'valve'), may hold values from -6 to 6
- bg_source: float32 [5, 32, 256, 128], P(None, 'bulk', 'valve'), may hold values from -6 to 6
- bg_iblank: int32 [32, 256, 128], P('bulk', 'valve'), may hold values 0 or 1
- valve_adjoint: float32 [5, 64, 128, 128], P(None, 'valve', 'bulk'), may hold values from -6 to 6
- valve_velocity: float32 [3, 64, 128, 128], P(None, 'valve', 'bulk'), may hold values from -6 to 6
- valve_source: float32 [5, 64, 128, 128], P(None, 'valve', 'bulk'), may hold values from -6 to 6
- flux_mix: float32 [3, 5, 5], replicated, may hold values from -2.5 to 2.5
- rec_cell: int32 [32, 32, 128], P(('bulk', 'valve')), may hold values from 0 to 32767
- donor_base: int32 [32, 32, 128], P(('bulk', 'valve')), may hold values from 0 to 28542, as said below
- donor_weight: float32 [8, 32, 32, 128], P(None, ('bulk', 'valve')), may hold values from 0 to 1, as said below
- slot_count: int32 [32, 32], P(('bulk', 'valve')), may hold values from 0 to 128, as said below
Outputs:
- bg_out: float32 [5, 32, 256, 128], P(None, 'bulk', 'valve')
- valve_out: float32 [5, 64, 128, 128], P(None, 'valve', 'bulk')
The draws below stay inside these ranges and needn't reach their ends.
Inputs may be any that keep to these rules, and one draw needn't show every extreme that they name: donor_base is a cell of the block whose neighbours at +1 along each of the three dimensions, alone and together, are in the same block; both ends of the range occur in every draw. `donor_weight`: the eight weights of a slot are non-negative and sum to one. `slot_count`: some owner takes 128 live slots from every sender.
All inputs are finite; a program needn't handle non-finite values. No bound on the sum of `bg_iblank` on one device may be relied on, other than what follows from the above.
Results may differ from the reference program's by a relative error of at most 0.0001.
Values sent between devices are 32-bit elements; how exact they have to be, the bound alone decides.
No kernel may reach another device: no remote copies, remote signals or barrier semaphores. Data moves between devices by JAX's collectives and lax.ppermute only.
A program may use at most 128 MiB of HBM per device.

```python
import jax
import jax.numpy as jnp
from jax import lax

NVAR = 5
ITERS = 4
CAP = 128
BX = 8
BY = 32
BZ = 128
VX = 8
VY = 32
VZ = 128
NBX = 32
NBY = 256
NVX = 64
NVY = 128
BCELLS = 32768
VCELLS = 32768
N_BULK = 4
N_VALVE = 8


def draw_donor_base(key, part):
    devices = N_BULK * N_VALVE
    first, second, third = jax.random.split(jax.random.fold_in(key, 11), 3)
    shape = (devices, devices, CAP)
    along_x = jax.random.randint(first, shape, 0, BX - 1)
    along_y = jax.random.randint(second, shape, 0, BY - 1)
    along_z = jax.random.randint(third, shape, 0, BZ - 1)
    flat = (along_x * BY + along_y) * BZ + along_z
    highest = ((BX - 2) * BY + BY - 2) * BZ + BZ - 2
    owners = jnp.arange(devices, dtype=jnp.int32)[None, :, None]
    slots = jnp.arange(CAP, dtype=jnp.int32)[None, None, :]
    last_slot = slots == CAP - 1
    flat = jnp.where(last_slot & (owners == 0), highest, flat)
    flat = jnp.where(last_slot & (owners == 1), 0, flat)
    return flat.astype(jnp.int32)


def draw_donor_weight(key, part):
    devices = N_BULK * N_VALVE
    fractions = jax.random.uniform(jax.random.fold_in(key, 23), (3, devices, devices, CAP), jnp.float32)
    weights = []
    for corner in range(8):
        picks = (corner // 4, corner // 2 % 2, corner % 2)
        factor = jnp.ones((devices, devices, CAP), jnp.float32)
        for direction in range(3):
            part_frac = fractions[direction]
            factor = factor * (part_frac if picks[direction] == 1 else 1.0 - part_frac)
        weights.append(factor)
    return jnp.stack(weights, axis=0).astype(jnp.float32)


def draw_slot_count(key, part):
    devices = N_BULK * N_VALVE
    first, second, third = jax.random.split(jax.random.fold_in(key, 37), 3)
    raw_counts = jax.random.randint(first, (devices, devices), 0, CAP + 1)
    loading = jax.random.randint(second, (devices,), 2, 5)
    counts = raw_counts * loading[None, :] // 4
    hottest = jax.random.randint(third, (), 0, devices)
    owners = jnp.arange(devices, dtype=jnp.int32)[None, :]
    return jnp.where(owners == hottest, CAP, counts).astype(jnp.int32)


def touch_ends(drawn, key, smallest, top_value):
    dims = drawn.shape
    index_at = [jax.random.randint(jax.random.fold_in(key, axis), (), 0, dims[axis]) for axis in range(len(dims))]
    drawn = drawn.at[tuple(index_at)].set(smallest)
    longest = dims.index(max(dims))
    index_at[longest] = (index_at[longest] + 1) % dims[longest]
    return drawn.at[tuple(index_at)].set(top_value)


def levels(key, extent, shards, least, top_value):
    gain, own = 1.0, jax.random.fold_in(key, 6)
    for axis_at, blocks in shards:
        heights = jnp.exp(jax.random.uniform(jax.random.fold_in(own, axis_at), (blocks,), jnp.float32, least / len(shards), top_value / len(shards)))
        gain = gain * jnp.repeat(heights, extent[axis_at] // blocks).reshape([-1 if axis == axis_at else 1 for axis in range(len(extent))])
    return gain


def centred(rng, extent, width, bound, pieces=(), kind=jnp.bfloat16):
    values = width * jax.random.normal(rng, extent, jnp.float32)
    if pieces:
        values = values * levels(rng, extent, pieces, -0.22, 0.18)
    return jnp.clip(values, -bound, bound).astype(kind)


def setup_inputs(seed: int = 0) -> dict:
    arg_keys = jax.random.split(jax.random.key(seed), 13)
    bg_adjoint = centred(arg_keys[0], (NVAR, NBX, NBY, BZ), 1.0, 6.0, ((1, 4), (2, 8)), jnp.float32)
    bg_velocity = centred(arg_keys[1], (3, NBX, NBY, BZ), 1.0, 6.0, ((1, 4), (2, 8)), jnp.float32)
    bg_source = centred(arg_keys[2], (NVAR, NBX, NBY, BZ), 1.0, 6.0, ((1, 4), (2, 8)), jnp.float32)
    bg_iblank = touch_ends((jax.random.randint(arg_keys[3], (NBX, NBY, BZ), 0, 8) < 7).astype(jnp.int32), jax.random.fold_in(arg_keys[3], 1), 0, 1)
    valve_adjoint = centred(arg_keys[4], (NVAR, NVX, NVY, VZ), 1.0, 6.0, ((1, 8), (2, 4)), jnp.float32)
    valve_velocity = centred(arg_keys[5], (3, NVX, NVY, VZ), 1.0, 6.0, ((1, 8), (2, 4)), jnp.float32)
    valve_source = centred(arg_keys[6], (NVAR, NVX, NVY, VZ), 1.0, 6.0, ((1, 8), (2, 4)), jnp.float32)
    flux_mix = centred(arg_keys[7], (3, NVAR, NVAR), NVAR ** -0.5, 2.5, (), jnp.float32)
    rec_cell = touch_ends(jax.random.randint(arg_keys[8], (N_BULK * N_VALVE, N_BULK * N_VALVE, CAP), 0, VX * VY * VZ), jax.random.fold_in(arg_keys[8], 1), 0, (VX * VY * VZ) - 1).astype(jnp.int32)
    donor_base = draw_donor_base(jax.random.fold_in(arg_keys[12], 71), 0)
    donor_weight = draw_donor_weight(jax.random.fold_in(arg_keys[12], 71), 0)
    slot_count = draw_slot_count(jax.random.fold_in(arg_keys[12], 71), 0)
    return dict(bg_adjoint=bg_adjoint, bg_velocity=bg_velocity, bg_source=bg_source, bg_iblank=bg_iblank, valve_adjoint=valve_adjoint, valve_velocity=valve_velocity, valve_source=valve_source, flux_mix=flux_mix, rec_cell=rec_cell, donor_base=donor_base, donor_weight=donor_weight, slot_count=slot_count)


def slopes_of(velocity):
    inverse_speed = lax.rsqrt(1.0 + lax.optimization_barrier(jnp.sum(velocity * velocity, axis=0)))
    return velocity * inverse_speed[None]

def update_cells(padded, slopes, source, blanking, flux_mix):
    beside_all = padded[:, 2:, 1:-1, 1:-1] + padded[:, :-2, 1:-1, 1:-1]
    beside_all = beside_all + padded[:, 1:-1, 2:, 1:-1] + padded[:, 1:-1, :-2, 1:-1]
    beside_all = beside_all + padded[:, 1:-1, 1:-1, 2:] + padded[:, 1:-1, 1:-1, :-2]
    centrals = (padded[:, :-2, 1:-1, 1:-1] - padded[:, 2:, 1:-1, 1:-1], padded[:, 1:-1, :-2, 1:-1] - padded[:, 1:-1, 2:, 1:-1], padded[:, 1:-1, 1:-1, :-2] - padded[:, 1:-1, 1:-1, 2:])
    transposed = jnp.zeros_like(beside_all)
    for direction in range(3):
        mixed = jnp.einsum('ji,jxyz->ixyz', flux_mix[direction], centrals[direction], precision=lax.Precision.HIGHEST)
        transposed = transposed + slopes[direction][None] * (0.5 * mixed)
    return blanking * (beside_all - transposed + source) / 12.0

def sweep_grid(adjoint, velocity, source, blanking, flux_mix):
    slopes = slopes_of(velocity)
    for repeat in range(ITERS):
        padded = jnp.pad(adjoint, ((0, 0), (1, 1), (1, 1), (1, 1)))
        adjoint = update_cells(padded, slopes, source, blanking, flux_mix)
    return adjoint

def reference(bg_adjoint, bg_velocity, bg_source, bg_iblank, valve_adjoint, valve_velocity, valve_source, flux_mix, rec_cell, donor_base, donor_weight, slot_count):
    devices = N_BULK * N_VALVE
    valve_out = sweep_grid(valve_adjoint, valve_velocity, valve_source, 1.0, flux_mix)
    blocks = valve_out.reshape(NVAR, N_VALVE, VX, N_BULK, VY, VZ).transpose(3, 1, 0, 2, 4, 5).reshape(devices, NVAR, VCELLS)
    values = jax.vmap(lambda block, chosen: block[:, chosen])(blocks, rec_cell)
    valid = (jnp.arange(CAP, dtype=jnp.int32)[None, None, :] < slot_count[:, :, None]).astype(jnp.float32)
    active = values * valid[:, None]
    owner_start = jnp.arange(devices, dtype=jnp.int32)[None, :, None] * BCELLS
    pushed = jnp.zeros((NVAR, devices * BCELLS), jnp.float32)
    for corner in range(8):
        step_x, step_y, step_z = (corner // 4, corner // 2 % 2, corner % 2)
        offset = step_x * BY * BZ + step_y * BZ + step_z
        target = (owner_start + donor_base + offset).reshape(-1).astype(jnp.int32)
        contrib = donor_weight[corner][:, None] * active
        pushed = pushed.at[:, target].add(contrib.transpose(1, 0, 2, 3).reshape(NVAR, -1))
    pushed = pushed.reshape(NVAR, N_BULK, N_VALVE, BX, BY, BZ).transpose(0, 1, 3, 2, 4, 5).reshape(NVAR, NBX, NBY, BZ)
    blanking = bg_iblank.astype(jnp.float32)[None]
    bg_out = sweep_grid(bg_adjoint, bg_velocity, bg_source, blanking, flux_mix) + pushed
    return (bg_out, valve_out)
```

```python
import functools

import jax
import jax.numpy as jnp
from jax import lax
from jax.experimental import pallas as pl
from jax.experimental.pallas import tpu as pltpu
from jax.sharding import PartitionSpec as P

NVAR = 5
ITERS = 4
CAP = 128
BX = 8
BY = 32
BZ = 128
PLANES = BX * BY
FACE = BY + BX
SEND_ROWS = 16
VMEM_LIMIT = 48 * 1024 * 1024

VMEM = pl.BlockSpec(memory_space=pltpu.VMEM)
SMEM = pl.BlockSpec(memory_space=pltpu.SMEM)


def params():
    return pltpu.CompilerParams(vmem_limit_bytes=VMEM_LIMIT)


def f32(*shape):
    return jax.ShapeDtypeStruct(shape, jnp.float32)


def swap_pairs(count, odd):
    return {i: (i + 1 if i % 2 == odd else i - 1) % count for i in range(count)}


def face_plans(bulk, valve):
    number = lambda b, v: b * valve + v
    plans = []
    for odd in (0, 1):
        swap = swap_pairs(bulk, odd)
        plans.append([(number(b, v), number(swap[b], v)) for b in range(bulk) for v in range(valve)])
    for odd in (0, 1):
        swap = swap_pairs(valve, odd)
        pairs = []
        for b in range(bulk):
            for v in range(valve):
                end = odd and v in (0, valve - 1)
                pairs.append((number(b, v), number(b ^ 1, v) if end else number(b, swap[v])))
        plans.append(pairs)
    return plans


def exchange(faces, plans):
    return [lax.ppermute(face, ("bulk", "valve"), plan) for face, plan in zip(faces, plans)]


def write_faces(info, bg, va, sends):
    for axis in range(2):
        flip = info[axis] % 2
        planes, rows = (bg, va) if axis == 0 else (va, bg)
        for swap in range(2):
            send = sends[2 * axis + swap]
            high = (flip == 0) if swap == 0 else (flip == 1)
            x_at = jnp.where(high, BX - 1, 0)
            for c in range(NVAR):
                send[c, 0:BY, :] = planes[c, x_at]
                for x in range(BX):
                    send[c, BY + x : BY + x + 1, :] = jnp.where(
                        high, rows[c, x, BY - 1 : BY, :], rows[c, x, 0:1, :]
                    )


def fill_padded(info, grid, axis_x, faces, padded):
    axis_y = 1 - axis_x
    for c in range(NVAR):
        for x in range(BX):
            padded[c, x + 1, 8 : 8 + BY, :] = grid[c, x]
    for axis in range(2):
        even, odd = faces[2 * axis], faces[2 * axis + 1]
        flip = info[axis] % 2
        not_first = info[axis] > 0
        not_last = info[axis] < info[2 + axis] - 1
        rows = slice(0, BY) if axis == axis_x else slice(BY, FACE)
        for c in range(NVAR):
            first, second = even[c, rows, :], odd[c, rows, :]
            low = jnp.where(jnp.logical_and(not_first, flip == 0), second, jnp.where(not_first, first, 0.0))
            high = jnp.where(jnp.logical_and(not_last, flip == 0), first, jnp.where(not_last, second, 0.0))
            if axis == axis_x:
                padded[c, 0, 8 : 8 + BY, :] = low
                padded[c, BX + 1, 8 : 8 + BY, :] = high
            else:
                for x in range(BX):
                    padded[c, x + 1, 7:8, :] = low[x : x + 1, :]
                    padded[c, x + 1, 8 + BY : 9 + BY, :] = high[x : x + 1, :]


def sweep(flux, padded, velocity, source, blanking, out):
    rows = 16
    depth = lax.broadcasted_iota(jnp.int32, (rows, BZ), 1)
    first, last = depth == 0, depth == BZ - 1

    def plane(x, carry):
        for part in range(BY // rows):
            y = part * rows
            here = slice(y, y + rows)
            vel = [velocity[d, x, here, :] for d in range(3)]
            speed = 1.0 + (vel[0] * vel[0] + vel[1] * vel[1] + vel[2] * vel[2])
            half = 0.5 * lax.rsqrt(speed)
            acc = [source[i, x, here, :] for i in range(NVAR)]
            for d in range(3):
                slope = half * vel[d]
                mixed = []
                for j in range(NVAR):
                    if d == 0:
                        low = padded[j, x, y + 8 : y + 8 + rows, :]
                        high = padded[j, x + 2, y + 8 : y + 8 + rows, :]
                    elif d == 1:
                        low = padded[j, x + 1, y + 7 : y + 7 + rows, :]
                        high = padded[j, x + 1, y + 9 : y + 9 + rows, :]
                    else:
                        mid = padded[j, x + 1, y + 8 : y + 8 + rows, :]
                        low = jnp.where(first, 0.0, pltpu.roll(mid, 1, 1))
                        high = jnp.where(last, 0.0, pltpu.roll(mid, BZ - 1, 1))
                    acc[j] = acc[j] + (low + high)
                    mixed.append(slope * (high - low))
                for i in range(NVAR):
                    for j in range(NVAR):
                        acc[i] = acc[i] + flux[d, j, i] * mixed[j]
            scale = 1.0 / 12.0
            if blanking is not None:
                scale = blanking[x, here, :].astype(jnp.float32) * scale
            for i in range(NVAR):
                out[i, x, here, :] = scale * acc[i]
        return carry

    lax.fori_loop(0, BX, plane, 0)


def faces_kernel(info, bg, va, *sends):
    write_faces(info, bg, va, sends)


def first_faces(info, bg, va):
    return pl.pallas_call(
        faces_kernel,
        out_shape=[f32(NVAR, FACE, BZ)] * 4,
        in_specs=[SMEM, VMEM, VMEM],
        out_specs=[VMEM] * 4,
        compiler_params=params(),
        name="first_faces",
    )(info, bg, va)


def sweep_kernel(which, want_faces, info, flux, *refs):
    refs = list(refs)
    grids = {}
    for name in which:
        size = 4 if name == "bg" else 3
        grids[name] = refs[:size]
        refs = refs[size:]
    faces, refs = refs[:4], refs[4:]
    outs = {name: refs[k] for k, name in enumerate(which)}
    refs = refs[len(which) :]
    sends = refs[:4] if want_faces else None
    padded = refs[-1]
    for name in which:
        fill_padded(info, grids[name][0], 0 if name == "bg" else 1, faces, padded)
        blanking = grids[name][3] if name == "bg" else None
        sweep(flux, padded, grids[name][1], grids[name][2], blanking, outs[name])
    if want_faces:
        write_faces(info, outs["bg"], outs["va"], sends)


def sweep_call(info, flux, grids, faces, want_faces):
    which = tuple(grids)
    operands = [array for name in which for array in grids[name]]
    outs = [f32(NVAR, BX, BY, BZ)] * len(which) + ([f32(NVAR, FACE, BZ)] * 4 if want_faces else [])
    return pl.pallas_call(
        functools.partial(sweep_kernel, which, want_faces),
        out_shape=outs,
        in_specs=[SMEM, SMEM] + [VMEM] * (len(operands) + 4),
        out_specs=[VMEM] * len(outs),
        scratch_shapes=[pltpu.VMEM((NVAR, BX + 2, BY + 16, BZ), jnp.float32)],
        compiler_params=params(),
        name="sweep_" + "_".join(which),
    )(info, flux, *operands, *faces)


def parts_of(value):
    high = value.astype(jnp.bfloat16)
    return high, (value - high.astype(jnp.float32)).astype(jnp.bfloat16)


def pick_kernel(group, owners, count, valve, cells, base, weight, payload, table):
    for v in range(NVAR):
        across = valve[v].reshape(PLANES, BZ).T
        high, low = parts_of(across)
        table[v * BZ : (v + 1) * BZ, 0:PLANES] = high
        table[v * BZ : (v + 1) * BZ, PLANES : 2 * PLANES] = low
    width = group * CAP
    plane_at = lax.broadcasted_iota(jnp.int32, (PLANES, CAP), 0)
    depth_at = lax.broadcasted_iota(jnp.int32, (BZ, CAP), 0)
    slot_at = lax.broadcasted_iota(jnp.int32, (1, CAP), 1)

    def step(index, carry):
        start = index * group
        hits = []
        for k in range(group):
            plane = cells[pl.ds(start + k, 1), :] // BZ
            hits.append(jnp.where(plane_at == plane, 1.0, 0.0).astype(jnp.bfloat16))
        hit = jnp.concatenate(hits, axis=1)
        both = jnp.concatenate([hit, hit], axis=0)
        rows = jnp.dot(table[...], both, preferred_element_type=jnp.float32)
        for k in range(group):
            owner = start + k
            depth = cells[pl.ds(owner, 1), :] % BZ
            here = depth_at == depth
            live = slot_at < count[0, owner]
            for v in range(NVAR):
                row = rows[v * BZ : (v + 1) * BZ, k * CAP : (k + 1) * CAP]
                value = jnp.sum(jnp.where(here, row, 0.0), axis=0, keepdims=True)
                payload[owner, 8 + v : 9 + v, :] = jnp.where(live, value, 0.0)
            for k8 in range(8):
                payload[owner, k8 : k8 + 1, :] = weight[k8, pl.ds(owner, 1), :]
            payload[owner, 13:14, :] = base[pl.ds(owner, 1), :].astype(jnp.float32)
            payload[owner, 14:16, :] = jnp.zeros((2, CAP), jnp.float32)
        return carry

    lax.fori_loop(0, owners // group, step, 0)


def pick(count, valve, cells, base, weight):
    owners = cells.shape[0]
    group = 4 if owners % 4 == 0 else 1
    return pl.pallas_call(
        functools.partial(pick_kernel, group, owners),
        out_shape=f32(owners, SEND_ROWS, CAP),
        in_specs=[SMEM] + [VMEM] * 4,
        out_specs=VMEM,
        scratch_shapes=[pltpu.VMEM((NVAR * BZ, 2 * PLANES), jnp.bfloat16)],
        compiler_params=params(),
        name="pick",
    )(count, valve, cells, base, weight)


def scatter_kernel(group, senders, arrived, swept, out, total, spread, placed):
    width = group * CAP
    plane_at = lax.broadcasted_iota(jnp.int32, (PLANES, CAP), 0)
    depth_at = lax.broadcasted_iota(jnp.int32, (BZ, CAP), 0)
    total[...] = jnp.zeros_like(total)

    def step(index, carry):
        start = index * group
        for k in range(group):
            sender = start + k
            cols = slice(k * CAP, (k + 1) * CAP)
            lows = slice(width + k * CAP, width + (k + 1) * CAP)
            anchor = arrived[sender, 13:14, :].astype(jnp.int32)
            delta = plane_at - anchor // BZ
            at = [delta == i * BY + j for i in range(2) for j in range(2)]
            for step_z in range(2):
                whole = jnp.zeros((PLANES, CAP), jnp.float32)
                for corner in range(4):
                    row = 2 * corner + step_z
                    whole = jnp.where(at[corner], arrived[sender, row : row + 1, :], whole)
                high, low = parts_of(whole)
                spread[step_z * PLANES : (step_z + 1) * PLANES, cols] = high
                spread[step_z * PLANES : (step_z + 1) * PLANES, lows] = low
            here = depth_at == anchor % BZ
            for v in range(NVAR):
                high, low = parts_of(arrived[sender, 8 + v : 9 + v, :])
                high, low = high.astype(jnp.float32), low.astype(jnp.float32)
                placed[v * BZ : (v + 1) * BZ, cols] = jnp.where(here, high, 0.0).astype(jnp.bfloat16)
                placed[v * BZ : (v + 1) * BZ, lows] = jnp.where(here, low, 0.0).astype(jnp.bfloat16)
        dims = (((1,), (1,)), ((), ()))
        first = lax.dot_general(
            spread[:, :width], placed[:, :width], dims, preferred_element_type=jnp.float32
        )
        second = lax.dot_general(
            spread[:, :width], placed[:, width:], dims, preferred_element_type=jnp.float32
        )
        third = lax.dot_general(
            spread[:, width:], placed[:, :width], dims, preferred_element_type=jnp.float32
        )
        total[...] += first + (second + third)
        return carry

    lax.fori_loop(0, senders // group, step, 0)
    depth = lax.broadcasted_iota(jnp.int32, (PLANES, BZ), 1)
    for v in range(NVAR):
        cols = slice(v * BZ, (v + 1) * BZ)
        upper = jnp.where(depth == 0, 0.0, pltpu.roll(total[PLANES:, cols], 1, 1))
        pushed = total[:PLANES, cols] + upper
        out[v] = swept[v] + pushed.reshape(BX, BY, BZ)


def scatter(arrived, swept):
    senders = arrived.shape[0]
    group = 4 if senders % 4 == 0 else 1
    return pl.pallas_call(
        functools.partial(scatter_kernel, group, senders),
        out_shape=f32(NVAR, BX, BY, BZ),
        in_specs=[VMEM, VMEM],
        out_specs=VMEM,
        scratch_shapes=[
            pltpu.VMEM((2 * PLANES, NVAR * BZ), jnp.float32),
            pltpu.VMEM((2 * PLANES, 2 * group * CAP), jnp.bfloat16),
            pltpu.VMEM((NVAR * BZ, 2 * group * CAP), jnp.bfloat16),
        ],
        compiler_params=params(),
        name="scatter",
    )(arrived, swept)


def body(
    bulk,
    valve,
    bg_adjoint,
    bg_velocity,
    bg_source,
    bg_iblank,
    valve_adjoint,
    valve_velocity,
    valve_source,
    flux_mix,
    rec_cell,
    donor_base,
    donor_weight,
    slot_count,
):
    plans = face_plans(bulk, valve)
    info = jnp.stack(
        [lax.axis_index("bulk"), lax.axis_index("valve"), jnp.int32(bulk), jnp.int32(valve)]
    ).astype(jnp.int32)
    bg, va = bg_adjoint, valve_adjoint
    faces = first_faces(info, bg, va)
    for repeat in range(ITERS - 1):
        arrived = exchange(faces, plans)
        grids = {"bg": (bg, bg_velocity, bg_source, bg_iblank), "va": (va, valve_velocity, valve_source)}
        bg, va, *faces = sweep_call(info, flux_mix, grids, arrived, True)
    arrived = exchange(faces, plans)
    (va,) = sweep_call(info, flux_mix, {"va": (va, valve_velocity, valve_source)}, arrived, False)
    payload = pick(slot_count, va, rec_cell[0], donor_base[0], donor_weight[:, 0])
    received = lax.all_to_all(payload, ("bulk", "valve"), split_axis=0, concat_axis=0, tiled=True)
    (bg,) = sweep_call(info, flux_mix, {"bg": (bg, bg_velocity, bg_source, bg_iblank)}, arrived, False)
    return (scatter(received, bg), va)


def solution(mesh):
    placed = (
        P(None, "bulk", "valve", None),
        P(None, "bulk", "valve", None),
        P(None, "bulk", "valve", None),
        P("bulk", "valve", None),
        P(None, "valve", "bulk", None),
        P(None, "valve", "bulk", None),
        P(None, "valve", "bulk", None),
        P(),
        P(("bulk", "valve"), None, None),
        P(("bulk", "valve"), None, None),
        P(None, ("bulk", "valve"), None, None),
        P(("bulk", "valve"), None),
    )
    return jax.shard_map(
        functools.partial(body, mesh.shape["bulk"], mesh.shape["valve"]),
        mesh=mesh,
        in_specs=placed,
        out_specs=(P(None, "bulk", "valve", None), P(None, "valve", "bulk", None)),
        check_vma=False,
    )
```

```python
import functools

import jax
import jax.numpy as jnp
from jax import lax
from jax.experimental import pallas as pl
from jax.experimental.pallas import tpu as pltpu
from jax.sharding import PartitionSpec as P

NVAR = 5
ITERS = 4
CAP = 128
BX = 8
BY = 32
BZ = 128
PLANES = BX * BY
FACE = BY + BX
SEND_ROWS = 16

VMEM = pl.BlockSpec(memory_space=pltpu.VMEM)
SMEM = pl.BlockSpec(memory_space=pltpu.SMEM)
HBM = pl.BlockSpec(memory_space=pltpu.HBM)


def params(mib):
    return pltpu.CompilerParams(vmem_limit_bytes=mib * 1024 * 1024)


def in_hbm(x):
    return pltpu.with_memory_space_constraint(x, pltpu.HBM)


def f32(*shape):
    return jax.ShapeDtypeStruct(shape, jnp.float32)


def swap_pairs(count, odd):
    return {i: (i + 1 if i % 2 == odd else i - 1) % count for i in range(count)}


def face_plans(bulk, valve):
    number = lambda b, v: b * valve + v
    plans = []
    for odd in (0, 1):
        swap = swap_pairs(bulk, odd)
        plans.append([(number(b, v), number(swap[b], v)) for b in range(bulk) for v in range(valve)])
    for odd in (0, 1):
        swap = swap_pairs(valve, odd)
        pairs = []
        for b in range(bulk):
            for v in range(valve):
                end = odd and v in (0, valve - 1)
                pairs.append((number(b, v), number(b ^ 1, v) if end else number(b, swap[v])))
        plans.append(pairs)
    return plans


def exchange(faces, plans):
    return [lax.ppermute(face, ("bulk", "valve"), plan) for face, plan in zip(faces, plans)]


def low_high(flip, even, odd):
    return jnp.where(flip == 0, odd, even), jnp.where(flip == 0, even, odd)


def own_faces(info, grid, axis_x, messages):
    faces = []
    for c in range(NVAR):
        sides = []
        for axis, rows in ((axis_x, slice(0, BY)), (1 - axis_x, slice(BY, FACE))):
            even, odd = messages[2 * axis], messages[2 * axis + 1]
            sides += low_high(info[axis] % 2, even[c, rows, :], odd[c, rows, :])
        faces.append(sides)
    return faces


def arrived_faces(info, axis_x, messages):
    faces = own_faces(info, None, axis_x, messages)
    for c in range(NVAR):
        for at, axis in ((0, axis_x), (2, 1 - axis_x)):
            faces[c][at] = jnp.where(info[axis] > 0, faces[c][at], 0.0)
            faces[c][at + 1] = jnp.where(info[axis] < info[2 + axis] - 1, faces[c][at + 1], 0.0)
    return faces


def send_faces(info, axis_x, faces, messages):
    for c in range(NVAR):
        for at, axis, rows in ((0, axis_x, slice(0, BY)), (2, 1 - axis_x, slice(BY, FACE))):
            low, high = faces[c][at : at + 2]
            even = info[axis] % 2 == 0
            messages[2 * axis][c, rows, :] = jnp.where(even, high, low)
            messages[2 * axis + 1][c, rows, :] = jnp.where(even, low, high)


def block_face(ref, c, side):
    if side == 0:
        return ref[c, 0:BY, :]
    if side == 1:
        return ref[c, PLANES - BY : PLANES, :]
    return ref[c, pl.ds(0 if side == 2 else BY - 1, BX, stride=BY), :]


def swept_faces(info, flux, axis_x, inner, velocity, blanking, messages):
    halos = arrived_faces(info, axis_x, messages)
    shares = []
    for side in range(4):
        d, sign = side // 2, 2.0 * (side % 2) - 1.0
        vel = [block_face(velocity, k, side) for k in range(3)]
        speed = 1.0 + (vel[0] * vel[0] + vel[1] * vel[1] + vel[2] * vel[2])
        slope = (0.5 * sign) * lax.rsqrt(speed) * vel[d]
        scale = 1.0 / 12.0
        if blanking is not None:
            scale = block_face(blanking, 0, side).astype(jnp.float32) * scale
        mixed = [slope * halos[j][side] for j in range(NVAR)]
        share = []
        for i in range(NVAR):
            total = halos[i][side]
            for j in range(NVAR):
                total = total + flux[d, j, i] * mixed[j]
            share.append(scale * total)
        shares.append(share)
    x_row = lax.broadcasted_iota(jnp.int32, (BY, BZ), 0)
    y_row = lax.broadcasted_iota(jnp.int32, (BX, BZ), 0)
    faces = []
    for c in range(NVAR):
        xs = [block_face(inner, c, side) + shares[side][c] for side in range(2)]
        ys = [block_face(inner, c, side) + shares[side][c] for side in range(2, 4)]
        for k, at in enumerate((0, BX - 1)):
            for m, row in enumerate((0, BY - 1)):
                xs[k] = xs[k] + jnp.where(x_row == row, shares[2 + m][c][at : at + 1, :], 0.0)
                ys[m] = ys[m] + jnp.where(y_row == at, shares[k][c][row : row + 1, :], 0.0)
        faces.append(xs + ys)
    return faces


def loads(pairs, sem):
    copies = []
    for source, target in pairs:
        part = []
        for c in range(source.shape[0]):
            at = sum(map(len, copies)) + c
            part.append(pltpu.make_async_copy(source.at[c], target.at[c], sem.at[at]))
        copies.append(part)
    return copies


def each(copies, act):
    for part in copies:
        for copy in part:
            getattr(copy, act)()


def first_kernel(info, bg, va, *refs):
    messages, bg_here, va_here, sem = refs[:4], refs[4], refs[5], refs[6]
    copies = loads([(bg, bg_here), (va, va_here)], sem)
    each(copies, "start")
    for axis_x, grid in ((0, bg_here), (1, va_here)):
        each(copies[axis_x : axis_x + 1], "wait")
        faces = [[block_face(grid, c, side) for side in range(4)] for c in range(NVAR)]
        send_faces(info, axis_x, faces, messages)


def first_faces(info, bg, va):
    return pl.pallas_call(
        first_kernel,
        out_shape=[f32(NVAR, FACE, BZ)] * 4 + [f32(NVAR, PLANES, BZ)] * 2,
        in_specs=[SMEM, HBM, HBM],
        out_specs=[VMEM] * 6,
        scratch_shapes=[pltpu.SemaphoreType.DMA((2 * NVAR,))],
        compiler_params=params(4),
        name="first_faces",
    )(info, in_hbm(bg), in_hbm(va))


def faces_kernel(info, flux, bg, bg_velocity, blanking, va, va_velocity, *messages):
    arrived, sends = messages[:4], messages[4:]
    faces = swept_faces(info, flux, 0, bg, bg_velocity, blanking, arrived)
    send_faces(info, 0, faces, sends)
    faces = swept_faces(info, flux, 1, va, va_velocity, None, arrived)
    send_faces(info, 1, faces, sends)


def next_faces(info, flux, bg, bg_velocity, blanking, va, va_velocity, arrived):
    return pl.pallas_call(
        faces_kernel,
        out_shape=[f32(NVAR, FACE, BZ)] * 4,
        in_specs=[SMEM, SMEM] + [VMEM] * 9,
        out_specs=[VMEM] * 4,
        compiler_params=params(4),
        name="next_faces",
    )(info, flux, bg, bg_velocity, blanking, va, va_velocity, *arrived)


def fill_padded(faces, grid, padded):
    edge = jnp.zeros((1, BZ), jnp.float32)
    plane = jnp.zeros((BY, BZ), jnp.float32)
    inside = slice(8, 8 + BY)
    for c in range(NVAR):
        padded[c, 0, inside, :] = plane
        padded[c, BX + 1, inside, :] = plane
        for x in range(BX):
            if 0 < x < BX - 1:
                padded[c, x + 1, inside, :] = grid[c, x * BY : (x + 1) * BY, :]
            else:
                padded[c, x + 1, inside, :] = faces[c][0 if x == 0 else 1]
            padded[c, x + 1, 7:8, :] = edge
            padded[c, x + 1, 8:9, :] = faces[c][2][x : x + 1, :]
            padded[c, x + 1, 7 + BY : 8 + BY, :] = faces[c][3][x : x + 1, :]
            padded[c, x + 1, 8 + BY : 9 + BY, :] = edge


def sweep(flux, padded, velocity, source, blanking, out):
    rows = 16
    depth = lax.broadcasted_iota(jnp.int32, (rows, BZ), 1)
    first, last = depth == 0, depth == BZ - 1

    def plane(x, carry):
        for part in range(BY // rows):
            y = part * rows
            here = pl.ds(pl.multiple_of(x * BY + y, rows), rows)
            vel = [velocity[d, here, :] for d in range(3)]
            speed = 1.0 + (vel[0] * vel[0] + vel[1] * vel[1] + vel[2] * vel[2])
            half = 0.5 * lax.rsqrt(speed)
            acc = [source[i, here, :] for i in range(NVAR)]
            for d in range(3):
                slope = half * vel[d]
                mixed = []
                for j in range(NVAR):
                    if d == 0:
                        low = padded[j, x, y + 8 : y + 8 + rows, :]
                        high = padded[j, x + 2, y + 8 : y + 8 + rows, :]
                    elif d == 1:
                        low = padded[j, x + 1, y + 7 : y + 7 + rows, :]
                        high = padded[j, x + 1, y + 9 : y + 9 + rows, :]
                    else:
                        mid = padded[j, x + 1, y + 8 : y + 8 + rows, :]
                        low = jnp.where(first, 0.0, pltpu.roll(mid, 1, 1))
                        high = jnp.where(last, 0.0, pltpu.roll(mid, BZ - 1, 1))
                    acc[j] = acc[j] + (low + high)
                    mixed.append(slope * (high - low))
                for i in range(NVAR):
                    for j in range(NVAR):
                        acc[i] = acc[i] + flux[d, j, i] * mixed[j]
            scale = 1.0 / 12.0
            if blanking is not None:
                scale = blanking[0, here, :].astype(jnp.float32) * scale
            for i in range(NVAR):
                out[i, here, :] = scale * acc[i]
        return carry

    lax.fori_loop(0, BX, plane, 0)


def sweep_kernel(info, flux, *refs):
    bg, bg_velocity, bg_source, blanking, va, va_velocity, va_source = refs[:7]
    messages, (bg_out, va_out, bg_padded, va_padded) = refs[7:11], refs[11:]
    fill_padded(own_faces(info, bg, 0, messages), bg, bg_padded)
    fill_padded(own_faces(info, va, 1, messages), va, va_padded)
    sweep(flux, bg_padded, bg_velocity, bg_source, blanking, bg_out)
    sweep(flux, va_padded, va_velocity, va_source, None, va_out)


def first_sweep_kernel(info, flux, bg, va, *refs):
    fixed, messages, outs = refs[:5], refs[5:9], refs[9:]
    bg_out, va_out, here = outs[0], outs[1], outs[2:7]
    bg_padded, va_padded, sem = outs[7:]
    copies = loads(list(zip(fixed, here)), sem)
    each(copies, "start")
    fill_padded(own_faces(info, bg, 0, messages), bg, bg_padded)
    fill_padded(own_faces(info, va, 1, messages), va, va_padded)
    each(copies[:3], "wait")
    sweep(flux, bg_padded, here[0], here[1], here[2], bg_out)
    each(copies[3:], "wait")
    sweep(flux, va_padded, here[3], here[4], None, va_out)


def sweep_cost():
    cells = BX * BY * BZ
    return pl.CostEstimate(flops=2 * cells * 230, bytes_accessed=4 * cells * 37, transcendentals=2 * cells)


def padded_scratch():
    return [pltpu.VMEM((NVAR, BX + 2, BY + 16, BZ), jnp.float32)] * 2


def first_sweep(info, flux, bg, va, bg_fixed, va_fixed, messages):
    fixed = (*bg_fixed, *va_fixed)
    outs = pl.pallas_call(
        first_sweep_kernel,
        out_shape=[f32(NVAR, PLANES, BZ)] * 2 + [jax.ShapeDtypeStruct(x.shape, x.dtype) for x in fixed],
        in_specs=[SMEM, SMEM] + [VMEM] * 2 + [HBM] * 5 + [VMEM] * 4,
        out_specs=[VMEM] * 7,
        scratch_shapes=padded_scratch() + [pltpu.SemaphoreType.DMA((sum(x.shape[0] for x in fixed),))],
        compiler_params=params(8),
        cost_estimate=sweep_cost(),
        name="first_sweep",
    )(info, flux, bg, va, *map(in_hbm, fixed), *messages)
    return outs[0], outs[1], tuple(outs[2:5]), tuple(outs[5:7])


def sweep_inner(info, flux, bg, va, messages):
    return pl.pallas_call(
        sweep_kernel,
        out_shape=[f32(NVAR, PLANES, BZ)] * 2,
        in_specs=[SMEM, SMEM] + [VMEM] * 11,
        out_specs=[VMEM] * 2,
        scratch_shapes=padded_scratch(),
        compiler_params=params(8),
        cost_estimate=sweep_cost(),
        name="sweep_inner",
    )(info, flux, *bg, *va, *messages)


def add_faces(faces, inner, out):
    for c in range(NVAR):
        out[c, BY : PLANES - BY, :] = inner[c, BY : PLANES - BY, :]
        out[c, 0:BY, :] = faces[c][0]
        out[c, PLANES - BY : PLANES, :] = faces[c][1]
        for side in (2, 3):
            for x in range(1, BX - 1):
                row = x * BY + (0 if side == 2 else BY - 1)
                out[c, row : row + 1, :] = faces[c][side][x : x + 1, :]


def parts_of(value):
    high = value.astype(jnp.bfloat16)
    return high, (value - high.astype(jnp.float32)).astype(jnp.bfloat16)


def pick_kernel(group, info, flux, inner, velocity, *refs):
    arrived, (count, cells, base, weight) = refs[:4], refs[4:8]
    valve, payload, done, table, hits, next_hits, cells_here, base_here, weight_here, sem = refs[8:]
    owners = cells.shape[0]
    loaded = loads([(weight, weight_here)], sem)
    loaded += [[pltpu.make_async_copy(cells, cells_here, sem.at[8])]]
    loaded += [[pltpu.make_async_copy(base, base_here, sem.at[9])]]
    each(loaded, "start")
    add_faces(swept_faces(info, flux, 1, inner, velocity, None, arrived), inner, done)
    stored = [[pltpu.make_async_copy(done, valve, sem.at[10])]]
    each(stored, "start")
    for v in range(NVAR):
        across = done[v].T
        high, low = parts_of(across)
        table[v * BZ : (v + 1) * BZ, 0:PLANES] = high
        table[v * BZ : (v + 1) * BZ, PLANES : 2 * PLANES] = low
    each(loaded, "wait")
    plane_at = lax.broadcasted_iota(jnp.int32, (PLANES, CAP), 0)
    depth_at = lax.broadcasted_iota(jnp.int32, (BZ, CAP), 0)
    slot_at = lax.broadcasted_iota(jnp.int32, (1, CAP), 1)
    steps = owners // group

    def find(index, target):
        for k in range(group):
            plane = lax.shift_right_logical(cells_here[pl.ds(index * group + k, 1), :], 7)
            hit = jnp.where(plane_at == plane, 1.0, 0.0).astype(jnp.bfloat16)
            target[0:PLANES, k * CAP : (k + 1) * CAP] = hit
            target[PLANES:, k * CAP : (k + 1) * CAP] = hit

    def fetch(source):
        return jnp.dot(table[...], source[...], preferred_element_type=jnp.float32)

    def put(index, rows):
        for k in range(group):
            owner = index * group + k
            here = depth_at == jnp.bitwise_and(cells_here[pl.ds(owner, 1), :], BZ - 1)
            live = slot_at < count[0, owner]
            for v in range(NVAR):
                row = rows[v * BZ : (v + 1) * BZ, k * CAP : (k + 1) * CAP]
                value = jnp.sum(jnp.where(here, row, 0.0), axis=0, keepdims=True)
                payload[owner, 8 + v : 9 + v, :] = jnp.where(live, value, 0.0)
            for corner in range(8):
                payload[owner, corner : corner + 1, :] = weight_here[corner, pl.ds(owner, 1), :]
            payload[owner, 13:14, :] = base_here[pl.ds(owner, 1), :].astype(jnp.float32)
            payload[owner, 14:16, :] = jnp.zeros((2, CAP), jnp.float32)

    find(0, hits)

    def step(pair, carry):
        one, two = 2 * pair, 2 * pair + 1
        rows_one = fetch(hits)
        find(two, next_hits)
        rows_two = fetch(next_hits)
        put(one, rows_one)
        find(jnp.minimum(two + 1, steps - 1), hits)
        put(two, rows_two)
        return carry

    lax.fori_loop(0, steps // 2, step, 0)
    each(stored, "wait")


def pick(info, flux, inner, velocity, arrived, count, cells, base, weight):
    owners = cells.shape[0]
    group = 4 if owners % 8 == 0 else 1
    slots = group * CAP
    return pl.pallas_call(
        functools.partial(pick_kernel, group),
        out_shape=[f32(NVAR, PLANES, BZ), f32(owners, SEND_ROWS, CAP)],
        in_specs=[SMEM, SMEM] + [VMEM] * 6 + [SMEM] + [HBM] * 3,
        out_specs=[HBM, VMEM],
        scratch_shapes=[
            pltpu.VMEM((NVAR, PLANES, BZ), jnp.float32),
            pltpu.VMEM((NVAR * BZ, 2 * PLANES), jnp.bfloat16),
            pltpu.VMEM((2 * PLANES, slots), jnp.bfloat16),
            pltpu.VMEM((2 * PLANES, slots), jnp.bfloat16),
            pltpu.VMEM(cells.shape, jnp.int32),
            pltpu.VMEM(base.shape, jnp.int32),
            pltpu.VMEM(weight.shape, jnp.float32),
            pltpu.SemaphoreType.DMA((11,)),
        ],
        compiler_params=params(20),
        name="pick",
    )(info, flux, inner, velocity, *arrived, in_hbm(count), in_hbm(cells), in_hbm(base), in_hbm(weight))


def scatter_kernel(group, info, flux, inner, velocity, blanking, *refs):
    arrived, received = refs[:4], refs[4]
    out, swept, total, spread, placed, next_spread, next_placed, sem = refs[5:]
    width = group * CAP
    steps = received.shape[0] // group
    tile = 16
    plane_at = lax.broadcasted_iota(jnp.int32, (PLANES // tile, tile, CAP), 0) * tile
    plane_at = plane_at + lax.broadcasted_iota(jnp.int32, (PLANES // tile, tile, CAP), 1)
    plane_at = plane_at.astype(jnp.float32).astype(jnp.bfloat16)
    depth_at = plane_at[: BZ // tile]
    zero = jnp.zeros((), jnp.bfloat16)

    def wide(row):
        return jnp.broadcast_to(row, (tile, CAP)).astype(jnp.bfloat16)[None]

    def wide_parts(row):
        high = row.astype(jnp.bfloat16).astype(jnp.float32)
        return wide(high), wide(row - high)

    def build(index, spread, placed):
        for k in range(group):
            sender = index * group + k
            cols = [slice(part * width + k * CAP, part * width + (k + 1) * CAP) for part in range(2)]
            anchor = received[sender, 13:14, :].astype(jnp.int32)
            plane = lax.shift_right_logical(anchor, 7)
            at = [plane_at == wide((plane + (i * BY + j)).astype(jnp.float32)) for i in range(2) for j in range(2)]
            for step_z in range(2):
                rows = slice(step_z * PLANES, (step_z + 1) * PLANES)
                high = low = zero
                for corner in range(4):
                    row = 2 * corner + step_z
                    high_row, low_row = wide_parts(received[sender, row : row + 1, :])
                    high = jnp.where(at[corner], high_row, high)
                    low = jnp.where(at[corner], low_row, low)
                spread[rows, cols[0]] = low.reshape(PLANES, CAP)
                spread[rows, cols[1]] = high.reshape(PLANES, CAP)
            here = depth_at == wide(jnp.bitwise_and(anchor, BZ - 1).astype(jnp.float32))
            for v in range(NVAR):
                rows = slice(v * BZ, (v + 1) * BZ)
                high_row, low_row = wide_parts(received[sender, 8 + v : 9 + v, :])
                placed[rows, cols[0]] = jnp.where(here, high_row, zero).reshape(BZ, CAP)
                placed[rows, cols[1]] = jnp.where(here, low_row, zero).reshape(BZ, CAP)

    def add(spread, placed):
        dims = (((1,), (1,)), ((), ()))
        high = placed[:, :width]
        both = jnp.concatenate([high, high], axis=1)
        product = lax.dot_general(both, spread[...], dims, preferred_element_type=jnp.float32)
        product = product + lax.dot_general(
            placed[:, width:], spread[:, width:], dims, preferred_element_type=jnp.float32
        )
        total[...] += product

    add_faces(swept_faces(info, flux, 0, inner, velocity, blanking, arrived), inner, swept)
    total[...] = jnp.zeros_like(total)
    build(0, spread, placed)

    def step(pair, carry):
        two = 2 * pair + 1
        add(spread, placed)
        build(two, next_spread, next_placed)
        add(next_spread, next_placed)
        build(jnp.minimum(two + 1, steps - 1), spread, placed)
        return carry

    lax.fori_loop(0, steps // 2, step, 0)
    depth = lax.broadcasted_iota(jnp.int32, (BZ, PLANES), 0)
    stored = [[pltpu.make_async_copy(swept.at[v], out.at[v], sem.at[v])] for v in range(NVAR)]
    for v in range(NVAR):
        rows = slice(v * BZ, (v + 1) * BZ)
        upper = jnp.where(depth == 0, 0.0, pltpu.roll(total[rows, PLANES:], 1, 0))
        swept[v] = swept[v] + (total[rows, :PLANES] + upper).T
        each(stored[v : v + 1], "start")
    each(stored, "wait")


def scatter(info, flux, inner, velocity, blanking, arrived, received):
    senders = received.shape[0]
    group = 4 if senders % 8 == 0 else 1
    columns = 2 * group * CAP
    return pl.pallas_call(
        functools.partial(scatter_kernel, group),
        out_shape=f32(NVAR, PLANES, BZ),
        in_specs=[SMEM, SMEM] + [VMEM] * 8,
        out_specs=HBM,
        scratch_shapes=[
            pltpu.VMEM((NVAR, PLANES, BZ), jnp.float32),
            pltpu.VMEM((NVAR * BZ, 2 * PLANES), jnp.float32),
            pltpu.VMEM((2 * PLANES, columns), jnp.bfloat16),
            pltpu.VMEM((NVAR * BZ, columns), jnp.bfloat16),
            pltpu.VMEM((2 * PLANES, columns), jnp.bfloat16),
            pltpu.VMEM((NVAR * BZ, columns), jnp.bfloat16),
            pltpu.SemaphoreType.DMA((NVAR,)),
        ],
        compiler_params=params(32),
        name="scatter",
    )(info, flux, inner, velocity, blanking, *arrived, received)


def body(
    bulk,
    valve,
    bg_adjoint,
    bg_velocity,
    bg_source,
    bg_iblank,
    valve_adjoint,
    valve_velocity,
    valve_source,
    flux_mix,
    rec_cell,
    donor_base,
    donor_weight,
    slot_count,
):
    plans = face_plans(bulk, valve)
    info = jnp.stack(
        [lax.axis_index("bulk"), lax.axis_index("valve"), jnp.int32(bulk), jnp.int32(valve)]
    ).astype(jnp.int32)
    flat = lambda block: block.reshape(-1, PLANES, BZ)
    bg, va = flat(bg_adjoint), flat(valve_adjoint)
    bg_fixed = (flat(bg_velocity), flat(bg_source), flat(bg_iblank))
    va_fixed = (flat(valve_velocity), flat(valve_source))
    *faces, bg, va = first_faces(info, bg, va)
    for repeat in range(ITERS):
        arrived = exchange(faces, plans)
        if repeat == 0:
            bg, va, bg_fixed, va_fixed = first_sweep(info, flux_mix, bg, va, bg_fixed, va_fixed, faces)
        else:
            bg, va = sweep_inner(info, flux_mix, (bg, *bg_fixed), (va, *va_fixed), faces)
        if repeat < ITERS - 1:
            faces = next_faces(info, flux_mix, bg, bg_fixed[0], bg_fixed[2], va, va_fixed[0], arrived)
    va, payload = pick(
        info, flux_mix, va, va_fixed[0], arrived, slot_count, rec_cell[0], donor_base[0], donor_weight[:, 0]
    )
    received = lax.all_to_all(payload, ("bulk", "valve"), split_axis=0, concat_axis=0, tiled=True)
    bg = scatter(info, flux_mix, bg, bg_fixed[0], bg_fixed[2], arrived, received)
    return (bg.reshape(bg_adjoint.shape), va.reshape(valve_adjoint.shape))


def solution(mesh):
    placed = (
        P(None, "bulk", "valve", None),
        P(None, "bulk", "valve", None),
        P(None, "bulk", "valve", None),
        P("bulk", "valve", None),
        P(None, "valve", "bulk", None),
        P(None, "valve", "bulk", None),
        P(None, "valve", "bulk", None),
        P(),
        P(("bulk", "valve"), None, None),
        P(("bulk", "valve"), None, None),
        P(None, ("bulk", "valve"), None, None),
        P(("bulk", "valve"), None),
    )
    return jax.shard_map(
        functools.partial(body, mesh.shape["bulk"], mesh.shape["valve"]),
        mesh=mesh,
        in_specs=placed,
        out_specs=(P(None, "bulk", "valve", None), P(None, "valve", "bulk", None)),
        check_vma=False,
    )
```

```python
import functools

import jax
import jax.numpy as jnp
from jax import lax
from jax.experimental import pallas as pl
from jax.experimental.pallas import tpu as pltpu
from jax.sharding import PartitionSpec as P

NVAR = 5
ITERS = 4
CAP = 128
BX = 8
BY = 32
BZ = 128
PLANES = BX * BY
FACE = BY + BX
STEP = BY + 16
SEND_ROWS = 14
RUN = 2
RUNS = BZ // RUN

VMEM = pl.BlockSpec(memory_space=pltpu.VMEM)
SMEM = pl.BlockSpec(memory_space=pltpu.SMEM)
HBM = pl.BlockSpec(memory_space=pltpu.HBM)


def params(mib):
    return pltpu.CompilerParams(vmem_limit_bytes=mib * 1024 * 1024)


def in_hbm(x):
    return pltpu.with_memory_space_constraint(x, pltpu.HBM)


def f32(*shape):
    return jax.ShapeDtypeStruct(shape, jnp.float32)


def swap_pairs(count, odd):
    return {i: (i + 1 if i % 2 == odd else i - 1) % count for i in range(count)}


def face_plans(bulk, valve):
    number = lambda b, v: b * valve + v
    plans = []
    for odd in (0, 1):
        swap = swap_pairs(bulk, odd)
        plans.append([(number(b, v), number(swap[b], v)) for b in range(bulk) for v in range(valve)])
    for odd in (0, 1):
        swap = swap_pairs(valve, odd)
        pairs = []
        for b in range(bulk):
            for v in range(valve):
                end = odd and v in (0, valve - 1)
                pairs.append((number(b, v), number(b ^ 1, v) if end else number(b, swap[v])))
        plans.append(pairs)
    return plans


def exchange(faces, plans):
    order = (2, 3, 0, 1)
    arrived = {k: lax.ppermute(faces[k], ("bulk", "valve"), plans[k]) for k in order}
    return [arrived[k] for k in range(4)]


def low_high(flip, even, odd):
    return jnp.where(flip == 0, odd, even), jnp.where(flip == 0, even, odd)


def own_faces(info, grid, axis_x, messages):
    faces = []
    for c in range(NVAR):
        sides = []
        for axis, rows in ((axis_x, slice(0, BY)), (1 - axis_x, slice(BY, FACE))):
            even, odd = messages[2 * axis], messages[2 * axis + 1]
            sides += low_high(info[axis] % 2, even[c, rows, :], odd[c, rows, :])
        faces.append(sides)
    return faces


def arrived_faces(info, axis_x, messages):
    faces = own_faces(info, None, axis_x, messages)
    for c in range(NVAR):
        for at, axis in ((0, axis_x), (2, 1 - axis_x)):
            faces[c][at] = jnp.where(info[axis] > 0, faces[c][at], 0.0)
            faces[c][at + 1] = jnp.where(info[axis] < info[2 + axis] - 1, faces[c][at + 1], 0.0)
    return faces


def send_faces(info, axis_x, faces, messages):
    for c in range(NVAR):
        for at, axis, rows in ((0, axis_x, slice(0, BY)), (2, 1 - axis_x, slice(BY, FACE))):
            low, high = faces[c][at : at + 2]
            even = info[axis] % 2 == 0
            messages[2 * axis][c, rows, :] = jnp.where(even, high, low)
            messages[2 * axis + 1][c, rows, :] = jnp.where(even, low, high)


def block_face(ref, c, side):
    if side == 0:
        return ref[c, 0:BY, :]
    if side == 1:
        return ref[c, PLANES - BY : PLANES, :]
    return ref[c, pl.ds(0 if side == 2 else BY - 1, BX, stride=BY), :]


def swept_faces(info, flux, axis_x, inner, velocity, blanking, messages):
    halos = arrived_faces(info, axis_x, messages)
    shares = []
    for side in range(4):
        d, sign = side // 2, 2.0 * (side % 2) - 1.0
        vel = [block_face(velocity, k, side) for k in range(3)]
        speed = 1.0 + (vel[0] * vel[0] + vel[1] * vel[1] + vel[2] * vel[2])
        slope = (0.5 * sign) * lax.rsqrt(speed) * vel[d]
        scale = 1.0 / 12.0
        if blanking is not None:
            scale = block_face(blanking, 0, side).astype(jnp.float32) * scale
        mixed = [slope * halos[j][side] for j in range(NVAR)]
        share = []
        for i in range(NVAR):
            total = halos[i][side]
            for j in range(NVAR):
                total = total + flux[d, j, i] * mixed[j]
            share.append(scale * total)
        shares.append(share)
    x_row = lax.broadcasted_iota(jnp.int32, (BY, BZ), 0)
    y_row = lax.broadcasted_iota(jnp.int32, (BX, BZ), 0)
    faces = []
    for c in range(NVAR):
        xs = [block_face(inner, c, side) + shares[side][c] for side in range(2)]
        ys = [block_face(inner, c, side) + shares[side][c] for side in range(2, 4)]
        for k, at in enumerate((0, BX - 1)):
            for m, row in enumerate((0, BY - 1)):
                xs[k] = xs[k] + jnp.where(x_row == row, shares[2 + m][c][at : at + 1, :], 0.0)
                ys[m] = ys[m] + jnp.where(y_row == at, shares[k][c][row : row + 1, :], 0.0)
        faces.append(xs + ys)
    return faces


def loads(pairs, sem):
    copies = []
    for source, target in pairs:
        part = []
        for c in range(source.shape[0]):
            at = sum(map(len, copies)) + c
            part.append(pltpu.make_async_copy(source.at[c], target.at[c], sem.at[at]))
        copies.append(part)
    return copies


def each(copies, act):
    for part in copies:
        for copy in part:
            getattr(copy, act)()


def first_kernel(info, bg, va, *refs):
    messages, bg_here, va_here, sem = refs[:4], refs[4], refs[5], refs[6]
    copies = loads([(bg, bg_here), (va, va_here)], sem)
    each(copies, "start")
    for axis_x, grid in ((0, bg_here), (1, va_here)):
        each(copies[axis_x : axis_x + 1], "wait")
        faces = [[block_face(grid, c, side) for side in range(4)] for c in range(NVAR)]
        send_faces(info, axis_x, faces, messages)


def first_faces(info, bg, va):
    return pl.pallas_call(
        first_kernel,
        out_shape=[f32(NVAR, FACE, BZ)] * 4 + [f32(NVAR, PLANES, BZ)] * 2,
        in_specs=[SMEM, HBM, HBM],
        out_specs=[VMEM] * 6,
        scratch_shapes=[pltpu.SemaphoreType.DMA((2 * NVAR,))],
        compiler_params=params(4),
        name="first_faces",
    )(info, in_hbm(bg), in_hbm(va))


def faces_kernel(info, flux, bg, bg_velocity, blanking, va, va_velocity, *messages):
    arrived, sends = messages[:4], messages[4:]
    faces = swept_faces(info, flux, 0, bg, bg_velocity, blanking, arrived)
    send_faces(info, 0, faces, sends)
    faces = swept_faces(info, flux, 1, va, va_velocity, None, arrived)
    send_faces(info, 1, faces, sends)


def next_faces(info, flux, bg, bg_velocity, blanking, va, va_velocity, arrived):
    return pl.pallas_call(
        faces_kernel,
        out_shape=[f32(NVAR, FACE, BZ)] * 4,
        in_specs=[SMEM, SMEM] + [VMEM] * 9,
        out_specs=[VMEM] * 4,
        compiler_params=params(4),
        name="next_faces",
    )(info, flux, bg, bg_velocity, blanking, va, va_velocity, *arrived)


def fill_padded(faces, grid, padded):
    zeros = jnp.zeros((BY, BZ), jnp.float32)
    for c in range(NVAR):
        for x in range(-1, BX + 1):
            if x in (-1, BX):
                plane = zeros
            elif x in (0, BX - 1):
                plane = faces[c][0 if x == 0 else 1]
            else:
                plane = grid[c, x * BY : (x + 1) * BY, :]
            padded[c, (x + 1) * STEP + 8 : (x + 1) * STEP + 8 + BY, :] = plane
        for row, face in ((7, zeros[:BX]), (8, faces[c][2]), (7 + BY, faces[c][3]), (8 + BY, zeros[:BX])):
            padded[c, pl.ds(STEP + row, BX, stride=STEP), :] = face


def sweep(flux, padded, velocity, source, blanking, out):
    depth = lax.broadcasted_iota(jnp.int32, (BY, BZ), 1)
    first, last = depth == 0, depth == BZ - 1
    for x in range(BX):
        here = slice(x * BY, (x + 1) * BY)

        def near(j, dx, dy):
            start = (x + 1 + dx) * STEP + 8 + dy
            return padded[j, start : start + BY, :]

        vel = [velocity[d, here, :] for d in range(3)]
        speed = 1.0 + (vel[0] * vel[0] + vel[1] * vel[1] + vel[2] * vel[2])
        half = 0.5 * lax.rsqrt(speed)
        acc = [source[i, here, :] for i in range(NVAR)]
        for d in range(3):
            slope = half * vel[d]
            mixed = []
            for j in range(NVAR):
                if d == 0:
                    low, high = near(j, -1, 0), near(j, 1, 0)
                elif d == 1:
                    low, high = near(j, 0, -1), near(j, 0, 1)
                else:
                    mid = near(j, 0, 0)
                    low = jnp.where(first, 0.0, pltpu.roll(mid, 1, 1))
                    high = jnp.where(last, 0.0, pltpu.roll(mid, BZ - 1, 1))
                acc[j] = acc[j] + (low + high)
                mixed.append(slope * (high - low))
            for i in range(NVAR):
                for j in range(NVAR):
                    acc[i] = acc[i] + flux[d, j, i] * mixed[j]
        scale = 1.0 / 12.0
        if blanking is not None:
            scale = blanking[0, here, :].astype(jnp.float32) * scale
        for i in range(NVAR):
            out[i, here, :] = scale * acc[i]


def sweep_kernel(info, flux, *refs):
    bg, bg_velocity, bg_source, blanking, va, va_velocity, va_source = refs[:7]
    messages, (bg_out, va_out, bg_padded, va_padded) = refs[7:11], refs[11:]
    fill_padded(own_faces(info, bg, 0, messages), bg, bg_padded)
    fill_padded(own_faces(info, va, 1, messages), va, va_padded)
    sweep(flux, bg_padded, bg_velocity, bg_source, blanking, bg_out)
    sweep(flux, va_padded, va_velocity, va_source, None, va_out)


def first_sweep_kernel(info, flux, bg, va, *refs):
    fixed, messages, outs = refs[:5], refs[5:9], refs[9:]
    bg_out, va_out, here = outs[0], outs[1], outs[2:7]
    bg_padded, va_padded, sem = outs[7:]
    copies = loads(list(zip(fixed, here)), sem)
    each(copies, "start")
    fill_padded(own_faces(info, bg, 0, messages), bg, bg_padded)
    fill_padded(own_faces(info, va, 1, messages), va, va_padded)
    each(copies[:3], "wait")
    sweep(flux, bg_padded, here[0], here[1], here[2], bg_out)
    each(copies[3:], "wait")
    sweep(flux, va_padded, here[3], here[4], None, va_out)


def sweep_cost():
    cells = BX * BY * BZ
    return pl.CostEstimate(flops=2 * cells * 230, bytes_accessed=4 * cells * 37, transcendentals=2 * cells)


def padded_scratch():
    return [pltpu.VMEM((NVAR, (BX + 2) * STEP, BZ), jnp.float32)] * 2


def first_sweep(info, flux, bg, va, bg_fixed, va_fixed, messages):
    fixed = (*bg_fixed, *va_fixed)
    outs = pl.pallas_call(
        first_sweep_kernel,
        out_shape=[f32(NVAR, PLANES, BZ)] * 2 + [jax.ShapeDtypeStruct(x.shape, x.dtype) for x in fixed],
        in_specs=[SMEM, SMEM] + [VMEM] * 2 + [HBM] * 5 + [VMEM] * 4,
        out_specs=[VMEM] * 7,
        scratch_shapes=padded_scratch() + [pltpu.SemaphoreType.DMA((sum(x.shape[0] for x in fixed),))],
        compiler_params=params(8),
        cost_estimate=sweep_cost(),
        name="first_sweep",
    )(info, flux, bg, va, *map(in_hbm, fixed), *messages)
    return outs[0], outs[1], tuple(outs[2:5]), tuple(outs[5:7])


def sweep_inner(info, flux, bg, va, messages):
    return pl.pallas_call(
        sweep_kernel,
        out_shape=[f32(NVAR, PLANES, BZ)] * 2,
        in_specs=[SMEM, SMEM] + [VMEM] * 11,
        out_specs=[VMEM] * 2,
        scratch_shapes=padded_scratch(),
        compiler_params=params(8),
        cost_estimate=sweep_cost(),
        name="sweep_inner",
    )(info, flux, *bg, *va, *messages)


def add_faces(faces, inner, out):
    for c in range(NVAR):
        out[c, BY : PLANES - BY, :] = inner[c, BY : PLANES - BY, :]
        out[c, 0:BY, :] = faces[c][0]
        out[c, PLANES - BY : PLANES, :] = faces[c][1]
        out[c, pl.ds(0, BX, stride=BY), :] = faces[c][2]
        out[c, pl.ds(BY - 1, BX, stride=BY), :] = faces[c][3]


def parts_of(value):
    high = value.astype(jnp.bfloat16)
    return high, (value - high.astype(jnp.float32)).astype(jnp.bfloat16)


def pick_kernel(group, info, flux, inner, velocity, *refs):
    arrived, (count, cells, base, weight) = refs[:4], refs[4:8]
    valve, payload, done, table, hits, next_hits, rows_even, rows_odd, sem = refs[8:]
    owners = cells.shape[0]
    add_faces(swept_faces(info, flux, 1, inner, velocity, None, arrived), inner, done)
    stored = [[pltpu.make_async_copy(done, valve, sem.at[0])]]
    each(stored, "start")
    for v in range(NVAR):
        across = done[v].T
        high, low = parts_of(across)
        table[v * BZ : (v + 1) * BZ, 0:PLANES] = high
        table[v * BZ : (v + 1) * BZ, PLANES : 2 * PLANES] = low
    plane_at = lax.broadcasted_iota(jnp.int32, (PLANES, CAP), 0)
    row_at = lax.broadcasted_iota(jnp.int32, (8, CAP), 0)
    slot_at = lax.broadcasted_iota(jnp.int32, (1, CAP), 1)
    steps = owners // group

    def find(index, target):
        for k in range(group):
            plane = lax.shift_right_logical(cells[pl.ds(index * group + k, 1), :], 7)
            hit = jnp.where(plane_at == plane, 1.0, 0.0).astype(jnp.bfloat16)
            target[0:PLANES, k * CAP : (k + 1) * CAP] = hit
            target[PLANES:, k * CAP : (k + 1) * CAP] = hit

    def fetch(source, target):
        target[...] = jnp.dot(table[...], source[...], preferred_element_type=jnp.float32)

    def put(index, rows):
        for k in range(group):
            owner = index * group + k
            depth = jnp.bitwise_and(cells[pl.ds(owner, 1), :], BZ - 1)
            live = slot_at < count[0, owner]
            offset = jnp.broadcast_to(depth, (8, CAP)) - row_at
            found = [jnp.zeros((8, CAP), jnp.float32)] * NVAR
            for z in range(0, BZ, 8):
                here = offset == z
                for v in range(NVAR):
                    row = rows[v * BZ + z : v * BZ + z + 8, k * CAP : (k + 1) * CAP]
                    found[v] = jnp.where(here, row, found[v])
            parts = [weight[corner, pl.ds(owner, 1), :] for corner in range(8)]
            parts += [jnp.where(live, jnp.sum(found[v], axis=0, keepdims=True), 0.0) for v in range(NVAR)]
            parts += [base[pl.ds(owner, 1), :].astype(jnp.float32)]
            for at, part in enumerate(parts):
                payload[owner, :, at * CAP : (at + 1) * CAP] = part

    find(0, hits)
    fetch(hits, rows_odd)

    def step(pair, carry):
        one, two = 2 * pair, 2 * pair + 1
        find(one, hits)
        fetch(hits, rows_even)
        put(jnp.maximum(one - 1, 0), rows_odd)
        find(two, next_hits)
        fetch(next_hits, rows_odd)
        put(one, rows_even)
        return carry

    lax.fori_loop(0, steps // 2, step, 0)
    put(steps - 1, rows_odd)
    each(stored, "wait")


def pick(info, flux, inner, velocity, arrived, count, cells, base, weight):
    owners = cells.shape[0]
    group = 4 if owners % 8 == 0 else 1
    slots = group * CAP
    return pl.pallas_call(
        functools.partial(pick_kernel, group),
        out_shape=[f32(NVAR, PLANES, BZ), f32(owners, 1, SEND_ROWS * CAP)],
        in_specs=[SMEM, SMEM] + [VMEM] * 6 + [SMEM] + [VMEM] * 3,
        out_specs=[HBM, VMEM],
        scratch_shapes=[
            pltpu.VMEM((NVAR, PLANES, BZ), jnp.float32),
            pltpu.VMEM((NVAR * BZ, 2 * PLANES), jnp.bfloat16),
            pltpu.VMEM((2 * PLANES, slots), jnp.bfloat16),
            pltpu.VMEM((2 * PLANES, slots), jnp.bfloat16),
            pltpu.VMEM((NVAR * BZ, slots), jnp.float32),
            pltpu.VMEM((NVAR * BZ, slots), jnp.float32),
            pltpu.SemaphoreType.DMA((1,)),
        ],
        compiler_params=params(20),
        name="pick",
    )(info, flux, inner, velocity, *arrived, in_hbm(count), cells, base, weight)


def scatter_kernel(group, info, flux, inner, velocity, blanking, *refs):
    arrived, received = refs[:4], refs[4]
    out, swept, total, across, spread, placed, next_spread, next_placed, sem = refs[5:]
    width = group * CAP
    steps = received.shape[0] // group
    tile = 16
    plane_at = lax.broadcasted_iota(jnp.int32, (PLANES // tile, tile, CAP), 0) * tile
    plane_at = plane_at + lax.broadcasted_iota(jnp.int32, (PLANES // tile, tile, CAP), 1)
    plane_at = plane_at.astype(jnp.float32).astype(jnp.bfloat16)
    run_at, y_at = plane_at[: RUNS // tile], plane_at[: BY // tile]
    zero = jnp.zeros((), jnp.bfloat16)

    def wide(row):
        return jnp.broadcast_to(row, (tile, CAP)).astype(jnp.bfloat16)[None]

    def wide_parts(row):
        high = row.astype(jnp.bfloat16).astype(jnp.float32)
        return wide(high), wide(row - high)

    def row(sender, at):
        return received[sender, :, at * CAP : (at + 1) * CAP]

    def build(index, spread, placed):
        for k in range(group):
            sender = index * group + k
            cols = [slice(part * width + k * CAP, part * width + (k + 1) * CAP) for part in range(2)]
            anchor = row(sender, 13).astype(jnp.int32)
            depth = jnp.bitwise_and(anchor, BZ - 1)
            place = jnp.bitwise_and(depth, RUN - 1)
            row_y = jnp.bitwise_and(lax.shift_right_logical(anchor, 7), BY - 1)
            row_x = wide(lax.shift_right_logical(anchor, 12).astype(jnp.float32))
            at_y = [y_at == wide((row_y + j).astype(jnp.float32)) for j in range(2)]
            at_x = [row_x == jnp.full((), x, jnp.bfloat16) for x in range(-1, BX)]
            for spot in range(RUN + 1):
                along_y = []
                for i in range(2):
                    high = low = zero
                    for j in range(2):
                        weight = jnp.where(place == spot, row(sender, 4 * i + 2 * j), 0.0)
                        weight = jnp.where(place == spot - 1, row(sender, 4 * i + 2 * j + 1), weight)
                        high_row, low_row = wide_parts(weight)
                        high = jnp.where(at_y[j], high_row, high)
                        low = jnp.where(at_y[j], low_row, low)
                    along_y.append((low, high))
                for x in range(BX):
                    rows = slice(spot * PLANES + x * BY, spot * PLANES + (x + 1) * BY)
                    for part in range(2):
                        value = jnp.where(at_x[x], along_y[1][part], zero)
                        value = jnp.where(at_x[x + 1], along_y[0][part], value)
                        spread[rows, cols[part]] = value.reshape(BY, CAP)
            here = run_at == wide(jnp.right_shift(depth, RUN.bit_length() - 1).astype(jnp.float32))
            for v in range(NVAR):
                rows = slice(v * RUNS, (v + 1) * RUNS)
                high_row, low_row = wide_parts(row(sender, 8 + v))
                placed[rows, cols[0]] = jnp.where(here, high_row, zero).reshape(RUNS, CAP)
                placed[rows, cols[1]] = jnp.where(here, low_row, zero).reshape(RUNS, CAP)

    def add(spread, placed):
        dims = (((1,), (1,)), ((), ()))
        high_spread = spread[:, width:]
        product = lax.dot_general(placed[:, :width], spread[:, :width], dims, preferred_element_type=jnp.float32)
        values = jnp.concatenate([placed[:, :width], placed[:, width:]], axis=0)
        both = lax.dot_general(values, high_spread, dims, preferred_element_type=jnp.float32)
        product = product + (both[: NVAR * RUNS] + both[NVAR * RUNS :])
        total[...] += product

    add_faces(swept_faces(info, flux, 0, inner, velocity, blanking, arrived), inner, swept)
    total[...] = jnp.zeros_like(total)
    build(0, spread, placed)

    def step(pair, carry):
        two = 2 * pair + 1
        add(spread, placed)
        build(two, next_spread, next_placed)
        add(next_spread, next_placed)
        build(jnp.minimum(two + 1, steps - 1), spread, placed)
        return carry

    lax.fori_loop(0, steps // 2, step, 0)
    run = lax.broadcasted_iota(jnp.int32, (RUNS, PLANES), 0)
    stored = [[pltpu.make_async_copy(swept.at[v], out.at[v], sem.at[v])] for v in range(NVAR)]
    for v in range(NVAR):
        rows = slice(v * RUNS, (v + 1) * RUNS)
        for spot in range(RUN):
            block = total[rows, spot * PLANES : (spot + 1) * PLANES]
            if spot == 0:
                after = pltpu.roll(total[rows, RUN * PLANES :], 1, 0)
                block = block + jnp.where(run == 0, 0.0, after)
            for half in range(PLANES // CAP):
                cols = slice(half * CAP, (half + 1) * CAP)
                across[half, pl.ds(spot, RUNS, stride=RUN), :] = block[:, cols]
        for half in range(PLANES // CAP):
            planes = slice(half * CAP, (half + 1) * CAP)
            swept[v, planes, :] = swept[v, planes, :] + across[half].T
        each(stored[v : v + 1], "start")
    each(stored, "wait")


def scatter(info, flux, inner, velocity, blanking, arrived, received):
    senders = received.shape[0]
    group = 4 if senders % 8 == 0 else 1
    columns = 2 * group * CAP
    return pl.pallas_call(
        functools.partial(scatter_kernel, group),
        out_shape=f32(NVAR, PLANES, BZ),
        in_specs=[SMEM, SMEM] + [VMEM] * 8,
        out_specs=HBM,
        scratch_shapes=[
            pltpu.VMEM((NVAR, PLANES, BZ), jnp.float32),
            pltpu.VMEM((NVAR * RUNS, (RUN + 1) * PLANES), jnp.float32),
            pltpu.VMEM((PLANES // CAP, BZ, CAP), jnp.float32),
            pltpu.VMEM(((RUN + 1) * PLANES, columns), jnp.bfloat16),
            pltpu.VMEM((NVAR * RUNS, columns), jnp.bfloat16),
            pltpu.VMEM(((RUN + 1) * PLANES, columns), jnp.bfloat16),
            pltpu.VMEM((NVAR * RUNS, columns), jnp.bfloat16),
            pltpu.SemaphoreType.DMA((NVAR,)),
        ],
        compiler_params=params(32),
        name="scatter",
    )(info, flux, inner, velocity, blanking, *arrived, received)


def body(
    bulk,
    valve,
    bg_adjoint,
    bg_velocity,
    bg_source,
    bg_iblank,
    valve_adjoint,
    valve_velocity,
    valve_source,
    flux_mix,
    rec_cell,
    donor_base,
    donor_weight,
    slot_count,
):
    plans = face_plans(bulk, valve)
    info = jnp.stack(
        [lax.axis_index("bulk"), lax.axis_index("valve"), jnp.int32(bulk), jnp.int32(valve)]
    ).astype(jnp.int32)
    flat = lambda block: block.reshape(-1, PLANES, BZ)
    bg, va = flat(bg_adjoint), flat(valve_adjoint)
    bg_fixed = (flat(bg_velocity), flat(bg_source), flat(bg_iblank))
    va_fixed = (flat(valve_velocity), flat(valve_source))
    *faces, bg, va = first_faces(info, bg, va)
    for repeat in range(ITERS):
        arrived = exchange(faces, plans)
        if repeat == 0:
            bg, va, bg_fixed, va_fixed = first_sweep(info, flux_mix, bg, va, bg_fixed, va_fixed, faces)
        else:
            bg, va = sweep_inner(info, flux_mix, (bg, *bg_fixed), (va, *va_fixed), faces)
        if repeat < ITERS - 1:
            faces = next_faces(info, flux_mix, bg, bg_fixed[0], bg_fixed[2], va, va_fixed[0], arrived)
    va, payload = pick(
        info, flux_mix, va, va_fixed[0], arrived, slot_count, rec_cell[0], donor_base[0], donor_weight[:, 0]
    )
    received = lax.all_to_all(payload, ("bulk", "valve"), split_axis=0, concat_axis=0, tiled=True)
    bg = scatter(info, flux_mix, bg, bg_fixed[0], bg_fixed[2], arrived, received)
    return (bg.reshape(bg_adjoint.shape), va.reshape(valve_adjoint.shape))


def solution(mesh):
    placed = (
        P(None, "bulk", "valve", None),
        P(None, "bulk", "valve", None),
        P(None, "bulk", "valve", None),
        P("bulk", "valve", None),
        P(None, "valve", "bulk", None),
        P(None, "valve", "bulk", None),
        P(None, "valve", "bulk", None),
        P(),
        P(("bulk", "valve"), None, None),
        P(("bulk", "valve"), None, None),
        P(None, ("bulk", "valve"), None, None),
        P(("bulk", "valve"), None),
    )
    return jax.shard_map(
        functools.partial(body, mesh.shape["bulk"], mesh.shape["valve"]),
        mesh=mesh,
        in_specs=placed,
        out_specs=(P(None, "bulk", "valve", None), P(None, "valve", "bulk", None)),
        check_vma=False,
    )
```

```python
import functools

import jax
import jax.numpy as jnp
from jax import lax
from jax.experimental import pallas as pl
from jax.experimental.pallas import tpu as pltpu
from jax.sharding import PartitionSpec as P

NVAR = 5
ITERS = 4
CAP = 128
BX = 8
BY = 32
BZ = 128
PLANES = BX * BY
FACE = BY + BX
STEP = BY + 16
SEND_ROWS = 14
RUN = 2
RUNS = BZ // RUN
PLACE = {(1, 0): 0, (1, 1): 1, (0, 1): 2, (0, 0): 3}

VMEM = pl.BlockSpec(memory_space=pltpu.VMEM)
SMEM = pl.BlockSpec(memory_space=pltpu.SMEM)
HBM = pl.BlockSpec(memory_space=pltpu.HBM)


def params(mib):
    return pltpu.CompilerParams(vmem_limit_bytes=mib * 1024 * 1024)


def in_hbm(x):
    return pltpu.with_memory_space_constraint(x, pltpu.HBM)


def f32(*shape):
    return jax.ShapeDtypeStruct(shape, jnp.float32)


def swap_pairs(count, odd):
    return {i: (i + 1 if i % 2 == odd else i - 1) % count for i in range(count)}


def face_plans(bulk, valve):
    number = lambda b, v: b * valve + v
    cells = [(b, v) for b in range(bulk) for v in range(valve)]
    plans = {}
    for odd in (0, 1):
        along_bulk, along_valve = swap_pairs(bulk, odd), swap_pairs(valve, odd)
        bulk_pairs, valve_pairs = [], []
        for b, v in cells:
            valve_end = odd and v in (0, valve - 1)
            bulk_pairs.append((number(b, v), number(along_bulk[b], v)))
            valve_pairs.append((number(b, v), number(b ^ 1, v) if valve_end else number(b, along_valve[v])))
        plans[0, odd], plans[1, odd] = bulk_pairs, valve_pairs
    return [plans[key] for key in sorted(PLACE, key=PLACE.get)]


def exchange(faces, plans):
    order = (2, 3, 0, 1)
    arrived = {k: lax.ppermute(faces[k], ("bulk", "valve"), plans[k]) for k in order}
    return [arrived[k] for k in range(4)]


def tall(tile, rows):
    return tile if rows == 8 else jnp.concatenate([tile] * (rows // 8), axis=0)


def flags(index, count):
    return [index % 2 == 0, index > 0, index < count - 1]


def flag(info, axis, which, rows):
    return tall(info[3 * axis + which], rows) != 0


def own_faces(info, axis_x, messages):
    faces = []
    for c in range(NVAR):
        sides = []
        for axis, start, size in ((axis_x, 0, BY), (1 - axis_x, BY, BX)):
            rows = slice(start, start + size)
            even, odd = messages[PLACE[axis, 0]][c, rows, :], messages[PLACE[axis, 1]][c, rows, :]
            is_even = flag(info, axis, 0, size)
            sides += [jnp.where(is_even, odd, even), jnp.where(is_even, even, odd)]
        faces.append(sides)
    return faces


def arrived_faces(info, axis_x, messages):
    faces = own_faces(info, axis_x, messages)
    for c in range(NVAR):
        for at, axis, size in ((0, axis_x, BY), (2, 1 - axis_x, BX)):
            for high in range(2):
                faces[c][at + high] = jnp.where(flag(info, axis, 1 + high, size), faces[c][at + high], 0.0)
    return faces


def send_faces(info, axis_x, faces, messages):
    for c in range(NVAR):
        for at, axis, start, size in ((0, axis_x, 0, BY), (2, 1 - axis_x, BY, BX)):
            rows = slice(start, start + size)
            low, high = faces[c][at : at + 2]
            is_even = flag(info, axis, 0, size)
            messages[PLACE[axis, 0]][c, rows, :] = jnp.where(is_even, high, low)
            messages[PLACE[axis, 1]][c, rows, :] = jnp.where(is_even, low, high)


def block_face(ref, c, side):
    if side == 0:
        return ref[c, 0:BY, :]
    if side == 1:
        return ref[c, PLANES - BY : PLANES, :]
    return ref[c, pl.ds(0 if side == 2 else BY - 1, BX, stride=BY), :]


def swept_faces(info, flux, axis_x, inner, velocity, blanking, messages):
    halos = arrived_faces(info, axis_x, messages)
    shares = []
    for side in range(4):
        d, sign = side // 2, 2.0 * (side % 2) - 1.0
        vel = [block_face(velocity, k, side) for k in range(3)]
        speed = 1.0 + (vel[0] * vel[0] + vel[1] * vel[1] + vel[2] * vel[2])
        slope = (0.5 * sign) * lax.rsqrt(speed) * vel[d]
        scale = 1.0 / 12.0
        if blanking is not None:
            scale = block_face(blanking, 0, side).astype(jnp.float32) * scale
        mixed = [slope * halos[j][side] for j in range(NVAR)]
        share = []
        for i in range(NVAR):
            total = halos[i][side]
            for j in range(NVAR):
                total = total + tall(flux[(d * NVAR + j) * NVAR + i], BY if d == 0 else BX) * mixed[j]
            share.append(scale * total)
        shares.append(share)
    x_row = lax.broadcasted_iota(jnp.int32, (BY, BZ), 0)
    y_row = lax.broadcasted_iota(jnp.int32, (BX, BZ), 0)
    faces = []
    for c in range(NVAR):
        xs = [block_face(inner, c, side) + shares[side][c] for side in range(2)]
        ys = [block_face(inner, c, side) + shares[side][c] for side in range(2, 4)]
        for k, at in enumerate((0, BX - 1)):
            for m, row in enumerate((0, BY - 1)):
                xs[k] = xs[k] + jnp.where(x_row == row, shares[2 + m][c][at : at + 1, :], 0.0)
                ys[m] = ys[m] + jnp.where(y_row == at, shares[k][c][row : row + 1, :], 0.0)
        faces.append(xs + ys)
    return faces


def loads(pairs, sem):
    copies = []
    for source, target in pairs:
        part = []
        for c in range(source.shape[0]):
            at = sum(map(len, copies)) + c
            part.append(pltpu.make_async_copy(source.at[c], target.at[c], sem.at[at]))
        copies.append(part)
    return copies


def each(copies, act):
    for part in copies:
        for copy in part:
            getattr(copy, act)()


def first_kernel(info, bg, va, *refs):
    messages, bg_here, va_here, sem = refs[:4], refs[4], refs[5], refs[6]
    copies = loads([(bg, bg_here), (va, va_here)], sem)
    each(copies, "start")
    for axis_x, grid in ((0, bg_here), (1, va_here)):
        each(copies[axis_x : axis_x + 1], "wait")
        faces = [[block_face(grid, c, side) for side in range(4)] for c in range(NVAR)]
        send_faces(info, axis_x, faces, messages)


def first_faces(info, bg, va):
    return pl.pallas_call(
        first_kernel,
        out_shape=[f32(NVAR, FACE, BZ)] * 4 + [f32(NVAR, PLANES, BZ)] * 2,
        in_specs=[VMEM, HBM, HBM],
        out_specs=[VMEM] * 6,
        scratch_shapes=[pltpu.SemaphoreType.DMA((2 * NVAR,))],
        compiler_params=params(4),
        name="first_faces",
    )(info, in_hbm(bg), in_hbm(va))


def faces_kernel(info, flux, bg, bg_velocity, blanking, va, va_velocity, *messages):
    arrived, sends = messages[:4], messages[4:]
    faces = swept_faces(info, flux, 0, bg, bg_velocity, blanking, arrived)
    send_faces(info, 0, faces, sends)
    faces = swept_faces(info, flux, 1, va, va_velocity, None, arrived)
    send_faces(info, 1, faces, sends)


def next_faces(info, flux, bg, bg_velocity, blanking, va, va_velocity, arrived):
    return pl.pallas_call(
        faces_kernel,
        out_shape=[f32(NVAR, FACE, BZ)] * 4,
        in_specs=[VMEM] * 11,
        out_specs=[VMEM] * 4,
        compiler_params=params(4),
        name="next_faces",
    )(info, flux, bg, bg_velocity, blanking, va, va_velocity, *arrived)


def fill_padded(faces, grid, padded):
    zeros = jnp.zeros((BY, BZ), jnp.float32)
    for c in range(NVAR):
        for x in range(-1, BX + 1):
            if x in (-1, BX):
                plane = zeros
            elif x in (0, BX - 1):
                plane = faces[c][0 if x == 0 else 1]
            else:
                plane = grid[c, x * BY : (x + 1) * BY, :]
            padded[c, (x + 1) * STEP + 8 : (x + 1) * STEP + 8 + BY, :] = plane
        for row, face in ((7, zeros[:BX]), (8, faces[c][2]), (7 + BY, faces[c][3]), (8 + BY, zeros[:BX])):
            padded[c, pl.ds(STEP + row, BX, stride=STEP), :] = face


def sweep(flux, padded, velocity, source, blanking, out):
    depth = lax.broadcasted_iota(jnp.int32, (BY, BZ), 1)
    first, last = depth == 0, depth == BZ - 1
    for x in range(BX):
        here = slice(x * BY, (x + 1) * BY)

        def near(j, dx, dy):
            start = (x + 1 + dx) * STEP + 8 + dy
            return padded[j, start : start + BY, :]

        vel = [velocity[d, here, :] for d in range(3)]
        speed = 1.0 + (vel[0] * vel[0] + vel[1] * vel[1] + vel[2] * vel[2])
        half = 0.5 * lax.rsqrt(speed)
        acc = [source[i, here, :] for i in range(NVAR)]
        for d in range(3):
            slope = half * vel[d]
            mixed = []
            for j in range(NVAR):
                if d == 0:
                    low, high = near(j, -1, 0), near(j, 1, 0)
                elif d == 1:
                    low, high = near(j, 0, -1), near(j, 0, 1)
                else:
                    mid = near(j, 0, 0)
                    low = jnp.where(first, 0.0, pltpu.roll(mid, 1, 1))
                    high = jnp.where(last, 0.0, pltpu.roll(mid, BZ - 1, 1))
                acc[j] = acc[j] + (low + high)
                mixed.append(slope * (high - low))
            for i in range(NVAR):
                for j in range(NVAR):
                    acc[i] = acc[i] + tall(flux[(d * NVAR + j) * NVAR + i], BY) * mixed[j]
        scale = 1.0 / 12.0
        if blanking is not None:
            scale = blanking[0, here, :].astype(jnp.float32) * scale
        for i in range(NVAR):
            out[i, here, :] = scale * acc[i]


def sweep_kernel(info, flux, *refs):
    bg, bg_velocity, bg_source, blanking, va, va_velocity, va_source = refs[:7]
    messages, (bg_out, va_out, bg_padded, va_padded) = refs[7:11], refs[11:]
    fill_padded(own_faces(info, 0, messages), bg, bg_padded)
    fill_padded(own_faces(info, 1, messages), va, va_padded)
    sweep(flux, bg_padded, bg_velocity, bg_source, blanking, bg_out)
    sweep(flux, va_padded, va_velocity, va_source, None, va_out)


def first_sweep_kernel(info, flux, bg, va, *refs):
    fixed, count, messages, outs = refs[:5], refs[5], refs[6:10], refs[10:]
    bg_out, va_out, here, wide, live = outs[0], outs[1], outs[2:7], outs[7], outs[8]
    bg_padded, va_padded, count_here, sem = outs[9:]
    copies = loads(list(zip(fixed, here)) + [(count, count_here)], sem)
    each(copies, "start")
    fill_padded(own_faces(info, 0, messages), bg, bg_padded)
    fill_padded(own_faces(info, 1, messages), va, va_padded)
    each(copies[:3], "wait")
    for d in range(3):
        for j in range(NVAR):
            for i in range(NVAR):
                wide[(d * NVAR + j) * NVAR + i] = jnp.broadcast_to(flux[d, j : j + 1, i : i + 1], (8, BZ))
    sweep(wide, bg_padded, here[0], here[1], here[2], bg_out)
    each(copies[3:], "wait")
    sweep(wide, va_padded, here[3], here[4], None, va_out)
    owners = count.shape[-1]
    counts = jnp.broadcast_to(count_here[0].astype(jnp.float32), (owners, owners))
    same = lax.broadcasted_iota(jnp.int32, (owners, owners), 0) == lax.broadcasted_iota(jnp.int32, (owners, owners), 1)
    counts = jnp.sum(jnp.where(same, counts, 0.0), axis=1, keepdims=True)
    slot_at = lax.broadcasted_iota(jnp.int32, (owners, CAP), 1).astype(jnp.float32)
    live[...] = jnp.where(slot_at < counts, 1.0, 0.0)


def sweep_cost():
    cells = BX * BY * BZ
    return pl.CostEstimate(flops=2 * cells * 230, bytes_accessed=4 * cells * 37, transcendentals=2 * cells)


def padded_scratch():
    return [pltpu.VMEM((NVAR, (BX + 2) * STEP, BZ), jnp.float32)] * 2


def first_sweep(info, flux, bg, va, bg_fixed, va_fixed, count, messages):
    fixed = (*bg_fixed, *va_fixed)
    outs = pl.pallas_call(
        first_sweep_kernel,
        out_shape=[f32(NVAR, PLANES, BZ)] * 2 + [jax.ShapeDtypeStruct(x.shape, x.dtype) for x in fixed]
        + [f32(3 * NVAR * NVAR, 8, BZ), f32(count.shape[-1], CAP)],
        in_specs=[VMEM] * 4 + [HBM] * 6 + [VMEM] * 4,
        out_specs=[VMEM] * 9,
        scratch_shapes=padded_scratch()
        + [pltpu.VMEM(count.shape, jnp.int32), pltpu.SemaphoreType.DMA((sum(x.shape[0] for x in fixed) + 1,))],
        compiler_params=params(8),
        cost_estimate=sweep_cost(),
        name="first_sweep",
    )(info, flux, bg, va, *map(in_hbm, (*fixed, count)), *messages)
    return outs[0], outs[1], tuple(outs[2:5]), tuple(outs[5:7]), outs[7], outs[8]


def sweep_inner(info, flux, bg, va, messages):
    return pl.pallas_call(
        sweep_kernel,
        out_shape=[f32(NVAR, PLANES, BZ)] * 2,
        in_specs=[VMEM] * 13,
        out_specs=[VMEM] * 2,
        scratch_shapes=padded_scratch(),
        compiler_params=params(8),
        cost_estimate=sweep_cost(),
        name="sweep_inner",
    )(info, flux, *bg, *va, *messages)


def add_faces(faces, inner, out):
    for c in range(NVAR):
        out[c, BY : PLANES - BY, :] = inner[c, BY : PLANES - BY, :]
        out[c, 0:BY, :] = faces[c][0]
        out[c, PLANES - BY : PLANES, :] = faces[c][1]
        out[c, pl.ds(0, BX, stride=BY), :] = faces[c][2]
        out[c, pl.ds(BY - 1, BX, stride=BY), :] = faces[c][3]


def parts_of(value):
    high = value.astype(jnp.bfloat16)
    return high, (value - high.astype(jnp.float32)).astype(jnp.bfloat16)


def pick_kernel(group, info, flux, inner, velocity, *refs):
    arrived, (live, cells, base, weight) = refs[:4], refs[4:8]
    valve, payload, done, table, hits, next_hits, rows_even, rows_odd, sem = refs[8:]
    owners = cells.shape[0]
    add_faces(swept_faces(info, flux, 1, inner, velocity, None, arrived), inner, done)
    stored = [[pltpu.make_async_copy(done, valve, sem.at[0])]]
    each(stored, "start")
    for v in range(NVAR):
        across = done[v].T
        high, low = parts_of(across)
        table[v * BZ : (v + 1) * BZ, 0:PLANES] = high
        table[v * BZ : (v + 1) * BZ, PLANES : 2 * PLANES] = low
    plane_at = lax.broadcasted_iota(jnp.int32, (PLANES, CAP), 0)
    row_at = lax.broadcasted_iota(jnp.int32, (8, CAP), 0)
    steps = owners // group

    def find(index, target):
        for k in range(group):
            plane = lax.shift_right_logical(cells[pl.ds(index * group + k, 1), :], 7)
            hit = jnp.where(plane_at == plane, 1.0, 0.0).astype(jnp.bfloat16)
            target[0:PLANES, k * CAP : (k + 1) * CAP] = hit
            target[PLANES:, k * CAP : (k + 1) * CAP] = hit

    def fetch(source, target):
        target[...] = jnp.dot(table[...], source[...], preferred_element_type=jnp.float32)

    def put(index, rows):
        for k in range(group):
            owner = index * group + k
            depth = jnp.bitwise_and(cells[pl.ds(owner, 1), :], BZ - 1)
            offset = jnp.broadcast_to(depth, (8, CAP)) - row_at
            found = [jnp.zeros((8, CAP), jnp.float32)] * NVAR
            for z in range(0, BZ, 8):
                here = offset == z
                for v in range(NVAR):
                    row = rows[v * BZ + z : v * BZ + z + 8, k * CAP : (k + 1) * CAP]
                    found[v] = jnp.where(here, row, found[v])
            parts = [weight[corner, pl.ds(owner, 1), :] for corner in range(8)]
            parts += [jnp.where(live[pl.ds(owner, 1), :] != 0.0, jnp.sum(found[v], axis=0, keepdims=True), 0.0) for v in range(NVAR)]
            parts += [base[pl.ds(owner, 1), :].astype(jnp.float32)]
            for at, part in enumerate(parts):
                payload[owner, :, at * CAP : (at + 1) * CAP] = part

    find(0, hits)
    fetch(hits, rows_odd)

    def step(pair, carry):
        one, two = 2 * pair, 2 * pair + 1
        find(one, hits)
        fetch(hits, rows_even)
        put(jnp.maximum(one - 1, 0), rows_odd)
        find(two, next_hits)
        fetch(next_hits, rows_odd)
        put(one, rows_even)
        return carry

    lax.fori_loop(0, steps // 2, step, 0)
    put(steps - 1, rows_odd)
    each(stored, "wait")


def pick(info, flux, inner, velocity, arrived, live, cells, base, weight):
    owners = cells.shape[0]
    group = 4 if owners % 8 == 0 else 1
    slots = group * CAP
    return pl.pallas_call(
        functools.partial(pick_kernel, group),
        out_shape=[f32(NVAR, PLANES, BZ), f32(owners, 1, SEND_ROWS * CAP)],
        in_specs=[VMEM] * 12,
        out_specs=[HBM, VMEM],
        scratch_shapes=[
            pltpu.VMEM((NVAR, PLANES, BZ), jnp.float32),
            pltpu.VMEM((NVAR * BZ, 2 * PLANES), jnp.bfloat16),
            pltpu.VMEM((2 * PLANES, slots), jnp.bfloat16),
            pltpu.VMEM((2 * PLANES, slots), jnp.bfloat16),
            pltpu.VMEM((NVAR * BZ, slots), jnp.float32),
            pltpu.VMEM((NVAR * BZ, slots), jnp.float32),
            pltpu.SemaphoreType.DMA((1,)),
        ],
        compiler_params=params(20),
        name="pick",
    )(info, flux, inner, velocity, *arrived, live, cells, base, weight)


def scatter_kernel(group, info, flux, inner, velocity, blanking, *refs):
    arrived, received = refs[:4], refs[4]
    out, swept, total, across, spread, placed, next_spread, next_placed, sem = refs[5:]
    width = group * CAP
    steps = received.shape[0] // group
    tile = 16
    plane_at = lax.broadcasted_iota(jnp.int32, (PLANES // tile, tile, CAP), 0) * tile
    plane_at = plane_at + lax.broadcasted_iota(jnp.int32, (PLANES // tile, tile, CAP), 1)
    plane_at = plane_at.astype(jnp.float32).astype(jnp.bfloat16)
    run_at, y_at = plane_at[: RUNS // tile], plane_at[: BY // tile]
    zero = jnp.zeros((), jnp.bfloat16)

    def wide(row):
        return jnp.broadcast_to(row, (tile, CAP)).astype(jnp.bfloat16)[None]

    def wide_parts(row):
        high = row.astype(jnp.bfloat16).astype(jnp.float32)
        return wide(high), wide(row - high)

    def row(sender, at):
        return received[sender, :, at * CAP : (at + 1) * CAP]

    def build(index, spread, placed):
        for k in range(group):
            sender = index * group + k
            cols = [slice(part * width + k * CAP, part * width + (k + 1) * CAP) for part in range(2)]
            anchor = row(sender, 13).astype(jnp.int32)
            depth = jnp.bitwise_and(anchor, BZ - 1)
            place = jnp.bitwise_and(depth, RUN - 1)
            row_y = jnp.bitwise_and(lax.shift_right_logical(anchor, 7), BY - 1)
            row_x = wide(lax.shift_right_logical(anchor, 12).astype(jnp.float32))
            at_y = [y_at == wide((row_y + j).astype(jnp.float32)) for j in range(2)]
            at_x = [row_x == jnp.full((), x, jnp.bfloat16) for x in range(-1, BX)]
            for spot in range(RUN + 1):
                along_y = []
                for i in range(2):
                    high = low = zero
                    for j in range(2):
                        weight = jnp.where(place == spot, row(sender, 4 * i + 2 * j), 0.0)
                        weight = jnp.where(place == spot - 1, row(sender, 4 * i + 2 * j + 1), weight)
                        high_row, low_row = wide_parts(weight)
                        high = jnp.where(at_y[j], high_row, high)
                        low = jnp.where(at_y[j], low_row, low)
                    along_y.append((low, high))
                for x in range(BX):
                    rows = slice(spot * PLANES + x * BY, spot * PLANES + (x + 1) * BY)
                    for part in range(2):
                        value = jnp.where(at_x[x], along_y[1][part], zero)
                        value = jnp.where(at_x[x + 1], along_y[0][part], value)
                        spread[rows, cols[part]] = value.reshape(BY, CAP)
            here = run_at == wide(jnp.right_shift(depth, RUN.bit_length() - 1).astype(jnp.float32))
            for v in range(NVAR):
                rows = slice(v * RUNS, (v + 1) * RUNS)
                high_row, low_row = wide_parts(row(sender, 8 + v))
                placed[rows, cols[0]] = jnp.where(here, high_row, zero).reshape(RUNS, CAP)
                placed[rows, cols[1]] = jnp.where(here, low_row, zero).reshape(RUNS, CAP)

    def add(spread, placed):
        dims = (((1,), (1,)), ((), ()))
        high_spread = spread[:, width:]
        product = lax.dot_general(placed[:, :width], spread[:, :width], dims, preferred_element_type=jnp.float32)
        values = jnp.concatenate([placed[:, :width], placed[:, width:]], axis=0)
        both = lax.dot_general(values, high_spread, dims, preferred_element_type=jnp.float32)
        product = product + (both[: NVAR * RUNS] + both[NVAR * RUNS :])
        total[...] += product

    add_faces(swept_faces(info, flux, 0, inner, velocity, blanking, arrived), inner, swept)
    total[...] = jnp.zeros_like(total)
    build(0, spread, placed)

    def step(pair, carry):
        two = 2 * pair + 1
        add(spread, placed)
        build(two, next_spread, next_placed)
        add(next_spread, next_placed)
        build(jnp.minimum(two + 1, steps - 1), spread, placed)
        return carry

    lax.fori_loop(0, steps // 2, step, 0)
    run = lax.broadcasted_iota(jnp.int32, (RUNS, PLANES), 0)
    stored = [[pltpu.make_async_copy(swept.at[v], out.at[v], sem.at[v])] for v in range(NVAR)]
    for v in range(NVAR):
        rows = slice(v * RUNS, (v + 1) * RUNS)
        for spot in range(RUN):
            block = total[rows, spot * PLANES : (spot + 1) * PLANES]
            if spot == 0:
                after = pltpu.roll(total[rows, RUN * PLANES :], 1, 0)
                block = block + jnp.where(run == 0, 0.0, after)
            for half in range(PLANES // CAP):
                cols = slice(half * CAP, (half + 1) * CAP)
                across[half, pl.ds(spot, RUNS, stride=RUN), :] = block[:, cols]
        for half in range(PLANES // CAP):
            planes = slice(half * CAP, (half + 1) * CAP)
            swept[v, planes, :] = swept[v, planes, :] + across[half].T
        each(stored[v : v + 1], "start")
    each(stored, "wait")


def scatter(info, flux, inner, velocity, blanking, arrived, received):
    senders = received.shape[0]
    group = 4 if senders % 8 == 0 else 1
    columns = 2 * group * CAP
    return pl.pallas_call(
        functools.partial(scatter_kernel, group),
        out_shape=f32(NVAR, PLANES, BZ),
        in_specs=[VMEM] * 10,
        out_specs=HBM,
        scratch_shapes=[
            pltpu.VMEM((NVAR, PLANES, BZ), jnp.float32),
            pltpu.VMEM((NVAR * RUNS, (RUN + 1) * PLANES), jnp.float32),
            pltpu.VMEM((PLANES // CAP, BZ, CAP), jnp.float32),
            pltpu.VMEM(((RUN + 1) * PLANES, columns), jnp.bfloat16),
            pltpu.VMEM((NVAR * RUNS, columns), jnp.bfloat16),
            pltpu.VMEM(((RUN + 1) * PLANES, columns), jnp.bfloat16),
            pltpu.VMEM((NVAR * RUNS, columns), jnp.bfloat16),
            pltpu.SemaphoreType.DMA((NVAR,)),
        ],
        compiler_params=params(32),
        name="scatter",
    )(info, flux, inner, velocity, blanking, *arrived, received)


def body(
    bulk,
    valve,
    bg_adjoint,
    bg_velocity,
    bg_source,
    bg_iblank,
    valve_adjoint,
    valve_velocity,
    valve_source,
    flux_mix,
    rec_cell,
    donor_base,
    donor_weight,
    slot_count,
):
    plans = face_plans(bulk, valve)
    info = flags(lax.axis_index("bulk"), bulk) + flags(lax.axis_index("valve"), valve)
    info = jnp.broadcast_to(jnp.stack(info).astype(jnp.int32)[:, None, None], (6, 8, BZ))
    flat = lambda block: block.reshape(-1, PLANES, BZ)
    bg, va = flat(bg_adjoint), flat(valve_adjoint)
    bg_fixed = (flat(bg_velocity), flat(bg_source), flat(bg_iblank))
    va_fixed = (flat(valve_velocity), flat(valve_source))
    *faces, bg, va = first_faces(info, bg, va)
    for repeat in range(ITERS):
        arrived = exchange(faces, plans)
        if repeat == 0:
            bg, va, bg_fixed, va_fixed, flux_wide, live = first_sweep(
                info, flux_mix, bg, va, bg_fixed, va_fixed, slot_count[:, None], faces
            )
        else:
            bg, va = sweep_inner(info, flux_wide, (bg, *bg_fixed), (va, *va_fixed), faces)
        if repeat < ITERS - 1:
            faces = next_faces(info, flux_wide, bg, bg_fixed[0], bg_fixed[2], va, va_fixed[0], arrived)
    va, payload = pick(
        info, flux_wide, va, va_fixed[0], arrived, live, rec_cell[0], donor_base[0], donor_weight[:, 0]
    )
    received = lax.all_to_all(payload, ("bulk", "valve"), split_axis=0, concat_axis=0, tiled=True)
    bg = scatter(info, flux_wide, bg, bg_fixed[0], bg_fixed[2], arrived, received)
    return (bg.reshape(bg_adjoint.shape), va.reshape(valve_adjoint.shape))


def solution(mesh):
    placed = (
        P(None, "bulk", "valve", None),
        P(None, "bulk", "valve", None),
        P(None, "bulk", "valve", None),
        P("bulk", "valve", None),
        P(None, "valve", "bulk", None),
        P(None, "valve", "bulk", None),
        P(None, "valve", "bulk", None),
        P(),
        P(("bulk", "valve"), None, None),
        P(("bulk", "valve"), None, None),
        P(None, ("bulk", "valve"), None, None),
        P(("bulk", "valve"), None),
    )
    return jax.shard_map(
        functools.partial(body, mesh.shape["bulk"], mesh.shape["valve"]),
        mesh=mesh,
        in_specs=placed,
        out_specs=(P(None, "bulk", "valve", None), P(None, "valve", "bulk", None)),
        check_vma=False,
    )
```

```python
import functools

import jax
import jax.numpy as jnp
from jax import lax
from jax.experimental import pallas as pl
from jax.experimental.pallas import tpu as pltpu
from jax.sharding import PartitionSpec as P

NVAR = 5
ITERS = 4
CAP = 128
BX = 8
BY = 32
BZ = 128
PLANES = BX * BY
FACE = BY + BX
STEP = BY + 16
SEND_ROWS = 13
RUN = 2
RUNS = BZ // RUN
PLACE = {(1, 0): 0, (1, 1): 1, (0, 1): 2, (0, 0): 3}

VMEM = pl.BlockSpec(memory_space=pltpu.VMEM)
SMEM = pl.BlockSpec(memory_space=pltpu.SMEM)
HBM = pl.BlockSpec(memory_space=pltpu.HBM)


def params(mib):
    return pltpu.CompilerParams(vmem_limit_bytes=mib * 1024 * 1024)


def in_hbm(x):
    return pltpu.with_memory_space_constraint(x, pltpu.HBM)


def f32(*shape):
    return jax.ShapeDtypeStruct(shape, jnp.float32)


def swap_pairs(count, odd):
    return {i: (i + 1 if i % 2 == odd else i - 1) % count for i in range(count)}


def face_plans(bulk, valve):
    number = lambda b, v: b * valve + v
    cells = [(b, v) for b in range(bulk) for v in range(valve)]
    plans = {}
    for odd in (0, 1):
        along_bulk, along_valve = swap_pairs(bulk, odd), swap_pairs(valve, odd)
        bulk_pairs, valve_pairs = [], []
        for b, v in cells:
            valve_end = odd and v in (0, valve - 1)
            bulk_pairs.append((number(b, v), number(along_bulk[b], v)))
            valve_pairs.append((number(b, v), number(b ^ 1, v) if valve_end else number(b, along_valve[v])))
        plans[0, odd], plans[1, odd] = bulk_pairs, valve_pairs
    return [plans[key] for key in sorted(PLACE, key=PLACE.get)]


def exchange(faces, plans):
    order = (2, 3, 0, 1)
    arrived = {k: lax.ppermute(faces[k], ("bulk", "valve"), plans[k]) for k in order}
    return [arrived[k] for k in range(4)]


def tall(tile, rows):
    return tile if rows == 8 else jnp.concatenate([tile] * (rows // 8), axis=0)


def flags(index, count):
    return [index % 2 == 0, index > 0, index < count - 1]


def flag(info, axis, which, rows):
    return tall(info[3 * axis + which], rows) != 0


def own_faces(info, axis_x, messages):
    faces = []
    for c in range(NVAR):
        sides = []
        for axis, start, size in ((axis_x, 0, BY), (1 - axis_x, BY, BX)):
            rows = slice(start, start + size)
            even, odd = messages[PLACE[axis, 0]][c, rows, :], messages[PLACE[axis, 1]][c, rows, :]
            is_even = flag(info, axis, 0, size)
            sides += [jnp.where(is_even, odd, even), jnp.where(is_even, even, odd)]
        faces.append(sides)
    return faces


def arrived_faces(info, axis_x, messages):
    faces = own_faces(info, axis_x, messages)
    for c in range(NVAR):
        for at, axis, size in ((0, axis_x, BY), (2, 1 - axis_x, BX)):
            for high in range(2):
                faces[c][at + high] = jnp.where(flag(info, axis, 1 + high, size), faces[c][at + high], 0.0)
    return faces


def send_faces(info, axis_x, faces, messages):
    for c in range(NVAR):
        for at, axis, start, size in ((0, axis_x, 0, BY), (2, 1 - axis_x, BY, BX)):
            rows = slice(start, start + size)
            low, high = faces[c][at : at + 2]
            is_even = flag(info, axis, 0, size)
            messages[PLACE[axis, 0]][c, rows, :] = jnp.where(is_even, high, low)
            messages[PLACE[axis, 1]][c, rows, :] = jnp.where(is_even, low, high)


def block_face(ref, c, side):
    if side == 0:
        return ref[c, 0:BY, :]
    if side == 1:
        return ref[c, PLANES - BY : PLANES, :]
    return ref[c, pl.ds(0 if side == 2 else BY - 1, BX, stride=BY), :]


def swept_faces(info, flux, axis_x, inner, velocity, blanking, messages):
    halos = arrived_faces(info, axis_x, messages)
    shares = []
    for side in range(4):
        d, sign = side // 2, 2.0 * (side % 2) - 1.0
        vel = [block_face(velocity, k, side) for k in range(3)]
        speed = 1.0 + (vel[0] * vel[0] + vel[1] * vel[1] + vel[2] * vel[2])
        slope = (0.5 * sign) * lax.rsqrt(speed) * vel[d]
        scale = 1.0 / 12.0
        if blanking is not None:
            scale = block_face(blanking, 0, side).astype(jnp.float32) * scale
        mixed = [slope * halos[j][side] for j in range(NVAR)]
        share = []
        for i in range(NVAR):
            total = halos[i][side]
            for j in range(NVAR):
                total = total + tall(flux[(d * NVAR + j) * NVAR + i], BY if d == 0 else BX) * mixed[j]
            share.append(scale * total)
        shares.append(share)
    x_row = lax.broadcasted_iota(jnp.int32, (BY, BZ), 0)
    y_row = lax.broadcasted_iota(jnp.int32, (BX, BZ), 0)
    faces = []
    for c in range(NVAR):
        xs = [block_face(inner, c, side) + shares[side][c] for side in range(2)]
        ys = [block_face(inner, c, side) + shares[side][c] for side in range(2, 4)]
        for k, at in enumerate((0, BX - 1)):
            for m, row in enumerate((0, BY - 1)):
                xs[k] = xs[k] + jnp.where(x_row == row, shares[2 + m][c][at : at + 1, :], 0.0)
                ys[m] = ys[m] + jnp.where(y_row == at, shares[k][c][row : row + 1, :], 0.0)
        faces.append(xs + ys)
    return faces


def loads(pairs, sem):
    copies = []
    for source, target in pairs:
        part = []
        for c in range(source.shape[0]):
            at = sum(map(len, copies)) + c
            part.append(pltpu.make_async_copy(source.at[c], target.at[c], sem.at[at]))
        copies.append(part)
    return copies


def each(copies, act):
    for part in copies:
        for copy in part:
            getattr(copy, act)()


def first_kernel(info, bg, va, *refs):
    messages, bg_here, va_here, sem = refs[:4], refs[4], refs[5], refs[6]
    copies = loads([(bg, bg_here), (va, va_here)], sem)
    each(copies, "start")
    for axis_x, grid in ((0, bg_here), (1, va_here)):
        each(copies[axis_x : axis_x + 1], "wait")
        faces = [[block_face(grid, c, side) for side in range(4)] for c in range(NVAR)]
        send_faces(info, axis_x, faces, messages)


def first_faces(info, bg, va):
    return pl.pallas_call(
        first_kernel,
        out_shape=[f32(NVAR, FACE, BZ)] * 4 + [f32(NVAR, PLANES, BZ)] * 2,
        in_specs=[VMEM, HBM, HBM],
        out_specs=[VMEM] * 6,
        scratch_shapes=[pltpu.SemaphoreType.DMA((2 * NVAR,))],
        compiler_params=params(4),
        name="first_faces",
    )(info, in_hbm(bg), in_hbm(va))


def faces_kernel(info, flux, bg, bg_velocity, blanking, va, va_velocity, *messages):
    arrived, sends = messages[:4], messages[4:]
    faces = swept_faces(info, flux, 0, bg, bg_velocity, blanking, arrived)
    send_faces(info, 0, faces, sends)
    faces = swept_faces(info, flux, 1, va, va_velocity, None, arrived)
    send_faces(info, 1, faces, sends)


def next_faces(info, flux, bg, bg_velocity, blanking, va, va_velocity, arrived):
    return pl.pallas_call(
        faces_kernel,
        out_shape=[f32(NVAR, FACE, BZ)] * 4,
        in_specs=[VMEM] * 11,
        out_specs=[VMEM] * 4,
        compiler_params=params(4),
        name="next_faces",
    )(info, flux, bg, bg_velocity, blanking, va, va_velocity, *arrived)


def fill_padded(faces, grid, padded):
    zeros = jnp.zeros((BY, BZ), jnp.float32)
    for c in range(NVAR):
        for x in range(-1, BX + 1):
            if x in (-1, BX):
                plane = zeros
            elif x in (0, BX - 1):
                plane = faces[c][0 if x == 0 else 1]
            else:
                plane = grid[c, x * BY : (x + 1) * BY, :]
            padded[c, (x + 1) * STEP + 8 : (x + 1) * STEP + 8 + BY, :] = plane
        for row, face in ((7, zeros[:BX]), (8, faces[c][2]), (7 + BY, faces[c][3]), (8 + BY, zeros[:BX])):
            padded[c, pl.ds(STEP + row, BX, stride=STEP), :] = face


def sweep(flux, padded, velocity, source, blanking, out):
    depth = lax.broadcasted_iota(jnp.int32, (BY, BZ), 1)
    first, last = depth == 0, depth == BZ - 1
    for x in range(BX):
        here = slice(x * BY, (x + 1) * BY)

        def near(j, dx, dy):
            start = (x + 1 + dx) * STEP + 8 + dy
            return padded[j, start : start + BY, :]

        vel = [velocity[d, here, :] for d in range(3)]
        speed = 1.0 + (vel[0] * vel[0] + vel[1] * vel[1] + vel[2] * vel[2])
        half = 0.5 * lax.rsqrt(speed)
        acc = [source[i, here, :] for i in range(NVAR)]
        for d in range(3):
            slope = half * vel[d]
            mixed = []
            for j in range(NVAR):
                if d == 0:
                    low, high = near(j, -1, 0), near(j, 1, 0)
                elif d == 1:
                    low, high = near(j, 0, -1), near(j, 0, 1)
                else:
                    mid = near(j, 0, 0)
                    low = jnp.where(first, 0.0, pltpu.roll(mid, 1, 1))
                    high = jnp.where(last, 0.0, pltpu.roll(mid, BZ - 1, 1))
                acc[j] = acc[j] + (low + high)
                mixed.append(slope * (high - low))
            for i in range(NVAR):
                for j in range(NVAR):
                    acc[i] = acc[i] + tall(flux[(d * NVAR + j) * NVAR + i], BY) * mixed[j]
        scale = 1.0 / 12.0
        if blanking is not None:
            scale = blanking[0, here, :].astype(jnp.float32) * scale
        for i in range(NVAR):
            out[i, here, :] = scale * acc[i]


def sweep_kernel(info, flux, *refs):
    bg, bg_velocity, bg_source, blanking, va, va_velocity, va_source = refs[:7]
    messages, (bg_out, va_out, bg_padded, va_padded) = refs[7:11], refs[11:]
    fill_padded(own_faces(info, 0, messages), bg, bg_padded)
    fill_padded(own_faces(info, 1, messages), va, va_padded)
    sweep(flux, bg_padded, bg_velocity, bg_source, blanking, bg_out)
    sweep(flux, va_padded, va_velocity, va_source, None, va_out)


def first_sweep_kernel(info, flux, bg, va, *refs):
    fixed, count, messages, outs = refs[:5], refs[5], refs[6:10], refs[10:]
    bg_out, va_out, here, wide, live = outs[0], outs[1], outs[2:7], outs[7], outs[8]
    bg_padded, va_padded, count_here, sem = outs[9:]
    copies = loads(list(zip(fixed, here)) + [(count, count_here)], sem)
    each(copies, "start")
    fill_padded(own_faces(info, 0, messages), bg, bg_padded)
    fill_padded(own_faces(info, 1, messages), va, va_padded)
    each(copies[:3], "wait")
    for d in range(3):
        for j in range(NVAR):
            for i in range(NVAR):
                wide[(d * NVAR + j) * NVAR + i] = jnp.broadcast_to(flux[d, j : j + 1, i : i + 1], (8, BZ))
    sweep(wide, bg_padded, here[0], here[1], here[2], bg_out)
    each(copies[3:], "wait")
    sweep(wide, va_padded, here[3], here[4], None, va_out)
    owners = count.shape[-1]
    counts = jnp.broadcast_to(count_here[0].astype(jnp.float32), (owners, owners))
    same = lax.broadcasted_iota(jnp.int32, (owners, owners), 0) == lax.broadcasted_iota(jnp.int32, (owners, owners), 1)
    counts = jnp.sum(jnp.where(same, counts, 0.0), axis=1, keepdims=True)
    slot_at = lax.broadcasted_iota(jnp.int32, (owners, CAP), 1).astype(jnp.float32)
    live[...] = jnp.where(slot_at < counts, 1.0, 0.0)


def sweep_cost():
    cells = BX * BY * BZ
    return pl.CostEstimate(flops=2 * cells * 230, bytes_accessed=4 * cells * 37, transcendentals=2 * cells)


def padded_scratch():
    return [pltpu.VMEM((NVAR, (BX + 2) * STEP, BZ), jnp.float32)] * 2


def first_sweep(info, flux, bg, va, bg_fixed, va_fixed, count, messages):
    fixed = (*bg_fixed, *va_fixed)
    outs = pl.pallas_call(
        first_sweep_kernel,
        out_shape=[f32(NVAR, PLANES, BZ)] * 2 + [jax.ShapeDtypeStruct(x.shape, x.dtype) for x in fixed]
        + [f32(3 * NVAR * NVAR, 8, BZ), f32(count.shape[-1], CAP)],
        in_specs=[VMEM] * 4 + [HBM] * 6 + [VMEM] * 4,
        out_specs=[VMEM] * 9,
        scratch_shapes=padded_scratch()
        + [pltpu.VMEM(count.shape, jnp.int32), pltpu.SemaphoreType.DMA((sum(x.shape[0] for x in fixed) + 1,))],
        compiler_params=params(8),
        cost_estimate=sweep_cost(),
        name="first_sweep",
    )(info, flux, bg, va, *map(in_hbm, (*fixed, count)), *messages)
    return outs[0], outs[1], tuple(outs[2:5]), tuple(outs[5:7]), outs[7], outs[8]


def sweep_inner(info, flux, bg, va, messages):
    return pl.pallas_call(
        sweep_kernel,
        out_shape=[f32(NVAR, PLANES, BZ)] * 2,
        in_specs=[VMEM] * 13,
        out_specs=[VMEM] * 2,
        scratch_shapes=padded_scratch(),
        compiler_params=params(8),
        cost_estimate=sweep_cost(),
        name="sweep_inner",
    )(info, flux, *bg, *va, *messages)


def add_faces(faces, inner, out):
    for c in range(NVAR):
        out[c, BY : PLANES - BY, :] = inner[c, BY : PLANES - BY, :]
        out[c, 0:BY, :] = faces[c][0]
        out[c, PLANES - BY : PLANES, :] = faces[c][1]
        out[c, pl.ds(0, BX, stride=BY), :] = faces[c][2]
        out[c, pl.ds(BY - 1, BX, stride=BY), :] = faces[c][3]


def parts_of(value):
    high = value.astype(jnp.bfloat16)
    return high, (value - high.astype(jnp.float32)).astype(jnp.bfloat16)


def pick_kernel(group, info, flux, inner, velocity, *refs):
    arrived, (live, cells, base, weight) = refs[:4], refs[4:8]
    valve, payload, done, table, hits, next_hits, rows_even, rows_odd, sem = refs[8:]
    owners = cells.shape[0]
    add_faces(swept_faces(info, flux, 1, inner, velocity, None, arrived), inner, done)
    stored = [[pltpu.make_async_copy(done, valve, sem.at[0])]]
    each(stored, "start")
    for v in range(NVAR):
        across = done[v].T
        high, low = parts_of(across)
        table[v * BZ : (v + 1) * BZ, 0:PLANES] = high
        table[v * BZ : (v + 1) * BZ, PLANES : 2 * PLANES] = low
    plane_at = lax.broadcasted_iota(jnp.int32, (PLANES, CAP), 0)
    row_at = lax.broadcasted_iota(jnp.int32, (8, CAP), 0)
    steps = owners // group

    def find(index, target):
        for k in range(group):
            plane = lax.shift_right_logical(cells[pl.ds(index * group + k, 1), :], 7)
            hit = jnp.where(plane_at == plane, 1.0, 0.0).astype(jnp.bfloat16)
            target[0:PLANES, k * CAP : (k + 1) * CAP] = hit
            target[PLANES:, k * CAP : (k + 1) * CAP] = hit

    def fetch(source, target):
        target[...] = jnp.dot(table[...], source[...], preferred_element_type=jnp.float32)

    def put(index, rows):
        for k in range(group):
            owner = index * group + k
            depth = jnp.bitwise_and(cells[pl.ds(owner, 1), :], BZ - 1)
            offset = jnp.broadcast_to(depth, (8, CAP)) - row_at
            found = [jnp.zeros((8, CAP), jnp.float32)] * NVAR
            for z in range(0, BZ, 8):
                here = offset == z
                for v in range(NVAR):
                    row = rows[v * BZ + z : v * BZ + z + 8, k * CAP : (k + 1) * CAP]
                    found[v] = jnp.where(here, row, found[v])
            parts = [weight[corner, pl.ds(owner, 1), :] for corner in range(7)]
            parts += [jnp.where(live[pl.ds(owner, 1), :] != 0.0, jnp.sum(found[v], axis=0, keepdims=True), 0.0) for v in range(NVAR)]
            parts += [base[pl.ds(owner, 1), :].astype(jnp.float32)]
            for at, part in enumerate(parts):
                payload[owner, :, at * CAP : (at + 1) * CAP] = part

    find(0, hits)
    fetch(hits, rows_even)
    find(1, next_hits)
    fetch(next_hits, rows_odd)
    put(0, rows_even)

    def step(pair, carry):
        one, two = 2 * pair, 2 * pair + 1
        find(one, hits)
        fetch(hits, rows_even)
        put(one - 1, rows_odd)
        find(two, next_hits)
        fetch(next_hits, rows_odd)
        put(one, rows_even)
        return carry

    lax.fori_loop(1, steps // 2, step, 0)
    put(steps - 1, rows_odd)
    each(stored, "wait")


def pick(info, flux, inner, velocity, arrived, live, cells, base, weight):
    owners = cells.shape[0]
    group = 4 if owners % 8 == 0 else 1
    slots = group * CAP
    return pl.pallas_call(
        functools.partial(pick_kernel, group),
        out_shape=[f32(NVAR, PLANES, BZ), f32(owners, 1, SEND_ROWS * CAP)],
        in_specs=[VMEM] * 12,
        out_specs=[HBM, VMEM],
        scratch_shapes=[
            pltpu.VMEM((NVAR, PLANES, BZ), jnp.float32),
            pltpu.VMEM((NVAR * BZ, 2 * PLANES), jnp.bfloat16),
            pltpu.VMEM((2 * PLANES, slots), jnp.bfloat16),
            pltpu.VMEM((2 * PLANES, slots), jnp.bfloat16),
            pltpu.VMEM((NVAR * BZ, slots), jnp.float32),
            pltpu.VMEM((NVAR * BZ, slots), jnp.float32),
            pltpu.SemaphoreType.DMA((1,)),
        ],
        compiler_params=params(20),
        name="pick",
    )(info, flux, inner, velocity, *arrived, live, cells, base, weight)


def scatter_kernel(group, info, flux, inner, velocity, blanking, *refs):
    arrived, received = refs[:4], refs[4]
    out, swept, total, across, spread, placed, next_spread, next_placed, sem = refs[5:]
    width = group * CAP
    steps = received.shape[0] // group
    tile = 16
    plane_at = lax.broadcasted_iota(jnp.int32, (PLANES // tile, tile, CAP), 0) * tile
    plane_at = plane_at + lax.broadcasted_iota(jnp.int32, (PLANES // tile, tile, CAP), 1)
    plane_at = plane_at.astype(jnp.float32).astype(jnp.bfloat16)
    run_at, y_at = plane_at[: RUNS // tile], plane_at[: BY // tile]
    zero = jnp.zeros((), jnp.bfloat16)

    def wide(row):
        return jnp.broadcast_to(row, (tile, CAP)).astype(jnp.bfloat16)[None]

    def wide_parts(row):
        high = row.astype(jnp.bfloat16).astype(jnp.float32)
        return wide(high), wide(row - high)

    def row(sender, at):
        return received[sender, :, at * CAP : (at + 1) * CAP]

    def build(index, spread, placed):
        for k in range(group):
            sender = index * group + k
            cols = [slice(part * width + k * CAP, part * width + (k + 1) * CAP) for part in range(2)]
            anchor = row(sender, 12).astype(jnp.int32)
            weights = [row(sender, corner) for corner in range(7)]
            weights.append(1.0 - sum(weights))
            depth = jnp.bitwise_and(anchor, BZ - 1)
            place = jnp.bitwise_and(depth, RUN - 1)
            row_y = jnp.bitwise_and(lax.shift_right_logical(anchor, 7), BY - 1)
            row_x = wide(lax.shift_right_logical(anchor, 12).astype(jnp.float32))
            at_y = [y_at == wide((row_y + j).astype(jnp.float32)) for j in range(2)]
            at_x = [row_x == jnp.full((), x, jnp.bfloat16) for x in range(-1, BX)]
            for spot in range(RUN + 1):
                along_y = []
                for i in range(2):
                    high = low = zero
                    for j in range(2):
                        weight = jnp.where(place == spot, weights[4 * i + 2 * j], 0.0)
                        weight = jnp.where(place == spot - 1, weights[4 * i + 2 * j + 1], weight)
                        high_row, low_row = wide_parts(weight)
                        high = jnp.where(at_y[j], high_row, high)
                        low = jnp.where(at_y[j], low_row, low)
                    along_y.append((low, high))
                for x in range(BX):
                    rows = slice(spot * PLANES + x * BY, spot * PLANES + (x + 1) * BY)
                    for part in range(2):
                        value = jnp.where(at_x[x], along_y[1][part], zero)
                        value = jnp.where(at_x[x + 1], along_y[0][part], value)
                        spread[rows, cols[part]] = value.reshape(BY, CAP)
            here = run_at == wide(jnp.right_shift(depth, RUN.bit_length() - 1).astype(jnp.float32))
            for v in range(NVAR):
                rows = slice(v * RUNS, (v + 1) * RUNS)
                high_row, low_row = wide_parts(row(sender, 7 + v))
                placed[rows, cols[0]] = jnp.where(here, high_row, zero).reshape(RUNS, CAP)
                placed[rows, cols[1]] = jnp.where(here, low_row, zero).reshape(RUNS, CAP)

    def add(spread, placed):
        dims = (((1,), (1,)), ((), ()))
        high_spread = spread[:, width:]
        product = lax.dot_general(placed[:, :width], spread[:, :width], dims, preferred_element_type=jnp.float32)
        values = jnp.concatenate([placed[:, :width], placed[:, width:]], axis=0)
        both = lax.dot_general(values, high_spread, dims, preferred_element_type=jnp.float32)
        product = product + (both[: NVAR * RUNS] + both[NVAR * RUNS :])
        total[...] += product

    total[...] = jnp.zeros_like(total)
    build(0, spread, placed)

    def step(pair, carry):
        add(spread, placed)
        build(2 * pair + 1, next_spread, next_placed)
        add(next_spread, next_placed)
        build(2 * pair + 2, spread, placed)
        return carry

    lax.fori_loop(0, steps // 2 - 1, step, 0)
    add(spread, placed)
    build(steps - 1, next_spread, next_placed)
    add_faces(swept_faces(info, flux, 0, inner, velocity, blanking, arrived), inner, swept)
    add(next_spread, next_placed)
    run = lax.broadcasted_iota(jnp.int32, (RUNS, PLANES), 0)
    stored = [[pltpu.make_async_copy(swept.at[v], out.at[v], sem.at[v])] for v in range(NVAR)]
    for v in range(NVAR):
        rows = slice(v * RUNS, (v + 1) * RUNS)
        for spot in range(RUN):
            block = total[rows, spot * PLANES : (spot + 1) * PLANES]
            if spot == 0:
                after = pltpu.roll(total[rows, RUN * PLANES :], 1, 0)
                block = block + jnp.where(run == 0, 0.0, after)
            for half in range(PLANES // CAP):
                cols = slice(half * CAP, (half + 1) * CAP)
                across[half, pl.ds(spot, RUNS, stride=RUN), :] = block[:, cols]
        for half in range(PLANES // CAP):
            planes = slice(half * CAP, (half + 1) * CAP)
            swept[v, planes, :] = swept[v, planes, :] + across[half].T
        each(stored[v : v + 1], "start")
    each(stored, "wait")


def scatter(info, flux, inner, velocity, blanking, arrived, received):
    senders = received.shape[0]
    group = 4 if senders % 8 == 0 else 1
    columns = 2 * group * CAP
    return pl.pallas_call(
        functools.partial(scatter_kernel, group),
        out_shape=f32(NVAR, PLANES, BZ),
        in_specs=[VMEM] * 10,
        out_specs=HBM,
        scratch_shapes=[
            pltpu.VMEM((NVAR, PLANES, BZ), jnp.float32),
            pltpu.VMEM((NVAR * RUNS, (RUN + 1) * PLANES), jnp.float32),
            pltpu.VMEM((PLANES // CAP, BZ, CAP), jnp.float32),
            pltpu.VMEM(((RUN + 1) * PLANES, columns), jnp.bfloat16),
            pltpu.VMEM((NVAR * RUNS, columns), jnp.bfloat16),
            pltpu.VMEM(((RUN + 1) * PLANES, columns), jnp.bfloat16),
            pltpu.VMEM((NVAR * RUNS, columns), jnp.bfloat16),
            pltpu.SemaphoreType.DMA((NVAR,)),
        ],
        compiler_params=params(32),
        name="scatter",
    )(info, flux, inner, velocity, blanking, *arrived, received)


def body(
    bulk,
    valve,
    bg_adjoint,
    bg_velocity,
    bg_source,
    bg_iblank,
    valve_adjoint,
    valve_velocity,
    valve_source,
    flux_mix,
    rec_cell,
    donor_base,
    donor_weight,
    slot_count,
):
    plans = face_plans(bulk, valve)
    info = flags(lax.axis_index("bulk"), bulk) + flags(lax.axis_index("valve"), valve)
    info = jnp.broadcast_to(jnp.stack(info).astype(jnp.int32)[:, None, None], (6, 8, BZ))
    flat = lambda block: block.reshape(-1, PLANES, BZ)
    bg, va = flat(bg_adjoint), flat(valve_adjoint)
    bg_fixed = (flat(bg_velocity), flat(bg_source), flat(bg_iblank))
    va_fixed = (flat(valve_velocity), flat(valve_source))
    *faces, bg, va = first_faces(info, bg, va)
    for repeat in range(ITERS):
        arrived = exchange(faces, plans)
        if repeat == 0:
            bg, va, bg_fixed, va_fixed, flux_wide, live = first_sweep(
                info, flux_mix, bg, va, bg_fixed, va_fixed, slot_count[:, None], faces
            )
        else:
            bg, va = sweep_inner(info, flux_wide, (bg, *bg_fixed), (va, *va_fixed), faces)
        if repeat < ITERS - 1:
            faces = next_faces(info, flux_wide, bg, bg_fixed[0], bg_fixed[2], va, va_fixed[0], arrived)
    va, payload = pick(
        info, flux_wide, va, va_fixed[0], arrived, live, rec_cell[0], donor_base[0], donor_weight[:, 0]
    )
    received = lax.all_to_all(payload, ("bulk", "valve"), split_axis=0, concat_axis=0, tiled=True)
    bg = scatter(info, flux_wide, bg, bg_fixed[0], bg_fixed[2], arrived, received)
    return (bg.reshape(bg_adjoint.shape), va.reshape(valve_adjoint.shape))


def solution(mesh):
    placed = (
        P(None, "bulk", "valve", None),
        P(None, "bulk", "valve", None),
        P(None, "bulk", "valve", None),
        P("bulk", "valve", None),
        P(None, "valve", "bulk", None),
        P(None, "valve", "bulk", None),
        P(None, "valve", "bulk", None),
        P(),
        P(("bulk", "valve"), None, None),
        P(("bulk", "valve"), None, None),
        P(None, ("bulk", "valve"), None, None),
        P(("bulk", "valve"), None),
    )
    return jax.shard_map(
        functools.partial(body, mesh.shape["bulk"], mesh.shape["valve"]),
        mesh=mesh,
        in_specs=placed,
        out_specs=(P(None, "bulk", "valve", None), P(None, "valve", "bulk", None)),
        check_vma=False,
    )
```

```python
import functools

import jax
import jax.numpy as jnp
from jax import lax
from jax.experimental import pallas as pl
from jax.experimental.pallas import tpu as pltpu
from jax.sharding import PartitionSpec as P

NVAR = 5
ITERS = 4
CAP = 128
BX = 8
BY = 32
BZ = 128
PLANES = BX * BY
FACE = BY + BX
STEP = BY + 16
SEND_ROWS = 13
RUN = 2
RUNS = BZ // RUN
PLACE = {(1, 0): 0, (1, 1): 1, (0, 1): 2, (0, 0): 3}

VMEM = pl.BlockSpec(memory_space=pltpu.VMEM)
SMEM = pl.BlockSpec(memory_space=pltpu.SMEM)
HBM = pl.BlockSpec(memory_space=pltpu.HBM)


def params(mib):
    return pltpu.CompilerParams(vmem_limit_bytes=mib * 1024 * 1024)


def in_hbm(x):
    return pltpu.with_memory_space_constraint(x, pltpu.HBM)


def f32(*shape):
    return jax.ShapeDtypeStruct(shape, jnp.float32)


def swap_pairs(count, odd):
    return {i: (i + 1 if i % 2 == odd else i - 1) % count for i in range(count)}


def face_plans(bulk, valve):
    number = lambda b, v: b * valve + v
    cells = [(b, v) for b in range(bulk) for v in range(valve)]
    plans = {}
    for odd in (0, 1):
        along_bulk, along_valve = swap_pairs(bulk, odd), swap_pairs(valve, odd)
        bulk_pairs, valve_pairs = [], []
        for b, v in cells:
            valve_end = odd and v in (0, valve - 1)
            bulk_pairs.append((number(b, v), number(along_bulk[b], v)))
            valve_pairs.append((number(b, v), number(b ^ 1, v) if valve_end else number(b, along_valve[v])))
        plans[0, odd], plans[1, odd] = bulk_pairs, valve_pairs
    return [plans[key] for key in sorted(PLACE, key=PLACE.get)]


def exchange(faces, plans):
    order = (2, 3, 0, 1)
    arrived = {k: lax.ppermute(faces[k], ("bulk", "valve"), plans[k]) for k in order}
    return [arrived[k] for k in range(4)]


def tall(tile, rows):
    return tile if rows == 8 else jnp.concatenate([tile] * (rows // 8), axis=0)


def flags(index, count):
    return [index % 2 == 0, index > 0, index < count - 1]


def flag(info, axis, which, rows):
    return tall(info[3 * axis + which], rows) != 0


def own_faces(info, axis_x, messages):
    faces = []
    for c in range(NVAR):
        sides = []
        for axis, start, size in ((axis_x, 0, BY), (1 - axis_x, BY, BX)):
            rows = slice(start, start + size)
            even, odd = messages[PLACE[axis, 0]][c, rows, :], messages[PLACE[axis, 1]][c, rows, :]
            is_even = flag(info, axis, 0, size)
            sides += [jnp.where(is_even, odd, even), jnp.where(is_even, even, odd)]
        faces.append(sides)
    return faces


def arrived_faces(info, axis_x, messages):
    faces = own_faces(info, axis_x, messages)
    for c in range(NVAR):
        for at, axis, size in ((0, axis_x, BY), (2, 1 - axis_x, BX)):
            for high in range(2):
                faces[c][at + high] = jnp.where(flag(info, axis, 1 + high, size), faces[c][at + high], 0.0)
    return faces


def send_faces(info, axis_x, faces, messages):
    for c in range(NVAR):
        for at, axis, start, size in ((0, axis_x, 0, BY), (2, 1 - axis_x, BY, BX)):
            rows = slice(start, start + size)
            low, high = faces[c][at : at + 2]
            is_even = flag(info, axis, 0, size)
            messages[PLACE[axis, 0]][c, rows, :] = jnp.where(is_even, high, low)
            messages[PLACE[axis, 1]][c, rows, :] = jnp.where(is_even, low, high)


def block_face(ref, c, side):
    if side == 0:
        return ref[c, 0:BY, :]
    if side == 1:
        return ref[c, PLANES - BY : PLANES, :]
    return ref[c, pl.ds(0 if side == 2 else BY - 1, BX, stride=BY), :]


def swept_faces(info, flux, axis_x, inner, velocity, blanking, messages):
    halos = arrived_faces(info, axis_x, messages)
    shares = []
    for side in range(4):
        d, sign = side // 2, 2.0 * (side % 2) - 1.0
        vel = [block_face(velocity, k, side) for k in range(3)]
        speed = 1.0 + (vel[0] * vel[0] + vel[1] * vel[1] + vel[2] * vel[2])
        slope = (0.5 * sign) * lax.rsqrt(speed) * vel[d]
        scale = 1.0 / 12.0
        if blanking is not None:
            scale = block_face(blanking, 0, side).astype(jnp.float32) * scale
        mixed = [slope * halos[j][side] for j in range(NVAR)]
        share = []
        for i in range(NVAR):
            total = halos[i][side]
            for j in range(NVAR):
                total = total + tall(flux[(d * NVAR + j) * NVAR + i], BY if d == 0 else BX) * mixed[j]
            share.append(scale * total)
        shares.append(share)
    x_row = lax.broadcasted_iota(jnp.int32, (BY, BZ), 0)
    y_row = lax.broadcasted_iota(jnp.int32, (BX, BZ), 0)
    faces = []
    for c in range(NVAR):
        xs = [block_face(inner, c, side) + shares[side][c] for side in range(2)]
        ys = [block_face(inner, c, side) + shares[side][c] for side in range(2, 4)]
        for k, at in enumerate((0, BX - 1)):
            for m, row in enumerate((0, BY - 1)):
                xs[k] = xs[k] + jnp.where(x_row == row, shares[2 + m][c][at : at + 1, :], 0.0)
                ys[m] = ys[m] + jnp.where(y_row == at, shares[k][c][row : row + 1, :], 0.0)
        faces.append(xs + ys)
    return faces


def loads(pairs, sem):
    copies = []
    for source, target in pairs:
        part = []
        for c in range(source.shape[0]):
            at = sum(map(len, copies)) + c
            part.append(pltpu.make_async_copy(source.at[c], target.at[c], sem.at[at]))
        copies.append(part)
    return copies


def each(copies, act):
    for part in copies:
        for copy in part:
            getattr(copy, act)()


def first_kernel(info, bg, va, *refs):
    messages, bg_here, va_here, sem = refs[:4], refs[4], refs[5], refs[6]
    copies = loads([(bg, bg_here), (va, va_here)], sem)
    each(copies, "start")
    for axis_x, grid in ((0, bg_here), (1, va_here)):
        each(copies[axis_x : axis_x + 1], "wait")
        faces = [[block_face(grid, c, side) for side in range(4)] for c in range(NVAR)]
        send_faces(info, axis_x, faces, messages)


def first_faces(info, bg, va):
    return pl.pallas_call(
        first_kernel,
        out_shape=[f32(NVAR, FACE, BZ)] * 4 + [f32(NVAR, PLANES, BZ)] * 2,
        in_specs=[VMEM, HBM, HBM],
        out_specs=[VMEM] * 6,
        scratch_shapes=[pltpu.SemaphoreType.DMA((2 * NVAR,))],
        compiler_params=params(4),
        name="first_faces",
    )(info, in_hbm(bg), in_hbm(va))


def faces_kernel(info, flux, bg, bg_velocity, blanking, va, va_velocity, *messages):
    arrived, sends = messages[:4], messages[4:]
    faces = swept_faces(info, flux, 0, bg, bg_velocity, blanking, arrived)
    send_faces(info, 0, faces, sends)
    faces = swept_faces(info, flux, 1, va, va_velocity, None, arrived)
    send_faces(info, 1, faces, sends)


def next_faces(info, flux, bg, bg_velocity, blanking, va, va_velocity, arrived):
    return pl.pallas_call(
        faces_kernel,
        out_shape=[f32(NVAR, FACE, BZ)] * 4,
        in_specs=[VMEM] * 11,
        out_specs=[VMEM] * 4,
        compiler_params=params(4),
        name="next_faces",
    )(info, flux, bg, bg_velocity, blanking, va, va_velocity, *arrived)


def fill_padded(faces, grid, padded):
    zeros = jnp.zeros((BY, BZ), jnp.float32)
    for c in range(NVAR):
        for x in range(-1, BX + 1):
            if x in (-1, BX):
                plane = zeros
            elif x in (0, BX - 1):
                plane = faces[c][0 if x == 0 else 1]
            else:
                plane = grid[c, x * BY : (x + 1) * BY, :]
            padded[c, (x + 1) * STEP + 8 : (x + 1) * STEP + 8 + BY, :] = plane
        for row, face in ((7, zeros[:BX]), (8, faces[c][2]), (7 + BY, faces[c][3]), (8 + BY, zeros[:BX])):
            padded[c, pl.ds(STEP + row, BX, stride=STEP), :] = face


def sweep(flux, padded, velocity, source, blanking, out):
    depth = lax.broadcasted_iota(jnp.int32, (BY, BZ), 1)
    first, last = depth == 0, depth == BZ - 1
    for x in range(BX):
        here = slice(x * BY, (x + 1) * BY)

        def near(j, dx, dy):
            start = (x + 1 + dx) * STEP + 8 + dy
            return padded[j, start : start + BY, :]

        vel = [velocity[d, here, :] for d in range(3)]
        speed = 1.0 + (vel[0] * vel[0] + vel[1] * vel[1] + vel[2] * vel[2])
        half = 0.5 * lax.rsqrt(speed)
        acc = [source[i, here, :] for i in range(NVAR)]
        for d in range(3):
            slope = half * vel[d]
            mixed = []
            for j in range(NVAR):
                if d == 0:
                    low, high = near(j, -1, 0), near(j, 1, 0)
                elif d == 1:
                    low, high = near(j, 0, -1), near(j, 0, 1)
                else:
                    mid = near(j, 0, 0)
                    low = jnp.where(first, 0.0, pltpu.roll(mid, 1, 1))
                    high = jnp.where(last, 0.0, pltpu.roll(mid, BZ - 1, 1))
                acc[j] = acc[j] + (low + high)
                mixed.append(slope * (high - low))
            for i in range(NVAR):
                for j in range(NVAR):
                    acc[i] = acc[i] + tall(flux[(d * NVAR + j) * NVAR + i], BY) * mixed[j]
        scale = 1.0 / 12.0
        if blanking is not None:
            scale = blanking[0, here, :].astype(jnp.float32) * scale
        for i in range(NVAR):
            out[i, here, :] = scale * acc[i]


def sweep_kernel(info, flux, *refs):
    bg, bg_velocity, bg_source, blanking, va, va_velocity, va_source = refs[:7]
    messages, (bg_out, va_out, bg_padded, va_padded) = refs[7:11], refs[11:]
    fill_padded(own_faces(info, 0, messages), bg, bg_padded)
    fill_padded(own_faces(info, 1, messages), va, va_padded)
    sweep(flux, bg_padded, bg_velocity, bg_source, blanking, bg_out)
    sweep(flux, va_padded, va_velocity, va_source, None, va_out)


def first_sweep_kernel(info, flux, bg, va, *refs):
    fixed, count, messages, outs = refs[:5], refs[5], refs[6:10], refs[10:]
    bg_out, va_out, here, wide, live = outs[0], outs[1], outs[2:7], outs[7], outs[8]
    bg_padded, va_padded, count_here, sem = outs[9:]
    copies = loads(list(zip(fixed, here)) + [(count, count_here)], sem)
    each(copies, "start")
    fill_padded(own_faces(info, 0, messages), bg, bg_padded)
    fill_padded(own_faces(info, 1, messages), va, va_padded)
    each(copies[:3], "wait")
    for d in range(3):
        for j in range(NVAR):
            for i in range(NVAR):
                wide[(d * NVAR + j) * NVAR + i] = jnp.broadcast_to(flux[d, j : j + 1, i : i + 1], (8, BZ))
    sweep(wide, bg_padded, here[0], here[1], here[2], bg_out)
    each(copies[3:], "wait")
    sweep(wide, va_padded, here[3], here[4], None, va_out)
    owners = count.shape[-1]
    counts = jnp.broadcast_to(count_here[0].astype(jnp.float32), (owners, owners))
    same = lax.broadcasted_iota(jnp.int32, (owners, owners), 0) == lax.broadcasted_iota(jnp.int32, (owners, owners), 1)
    counts = jnp.sum(jnp.where(same, counts, 0.0), axis=1, keepdims=True)
    slot_at = lax.broadcasted_iota(jnp.int32, (owners, CAP), 1).astype(jnp.float32)
    live[...] = jnp.where(slot_at < counts, 1.0, 0.0)


def sweep_cost():
    cells = BX * BY * BZ
    return pl.CostEstimate(flops=2 * cells * 230, bytes_accessed=4 * cells * 37, transcendentals=2 * cells)


def padded_scratch():
    return [pltpu.VMEM((NVAR, (BX + 2) * STEP, BZ), jnp.float32)] * 2


def first_sweep(info, flux, bg, va, bg_fixed, va_fixed, count, messages):
    fixed = (*bg_fixed, *va_fixed)
    outs = pl.pallas_call(
        first_sweep_kernel,
        out_shape=[f32(NVAR, PLANES, BZ)] * 2 + [jax.ShapeDtypeStruct(x.shape, x.dtype) for x in fixed]
        + [f32(3 * NVAR * NVAR, 8, BZ), f32(count.shape[-1], CAP)],
        in_specs=[VMEM] * 4 + [HBM] * 6 + [VMEM] * 4,
        out_specs=[VMEM] * 9,
        scratch_shapes=padded_scratch()
        + [pltpu.VMEM(count.shape, jnp.int32), pltpu.SemaphoreType.DMA((sum(x.shape[0] for x in fixed) + 1,))],
        compiler_params=params(8),
        cost_estimate=sweep_cost(),
        name="first_sweep",
    )(info, flux, bg, va, *map(in_hbm, (*fixed, count)), *messages)
    return outs[0], outs[1], tuple(outs[2:5]), tuple(outs[5:7]), outs[7], outs[8]


def sweep_inner(info, flux, bg, va, messages):
    return pl.pallas_call(
        sweep_kernel,
        out_shape=[f32(NVAR, PLANES, BZ)] * 2,
        in_specs=[VMEM] * 13,
        out_specs=[VMEM] * 2,
        scratch_shapes=padded_scratch(),
        compiler_params=params(8),
        cost_estimate=sweep_cost(),
        name="sweep_inner",
    )(info, flux, *bg, *va, *messages)


def add_faces(faces, inner, out):
    for c in range(NVAR):
        out[c, BY : PLANES - BY, :] = inner[c, BY : PLANES - BY, :]
        out[c, 0:BY, :] = faces[c][0]
        out[c, PLANES - BY : PLANES, :] = faces[c][1]
        out[c, pl.ds(0, BX, stride=BY), :] = faces[c][2]
        out[c, pl.ds(BY - 1, BX, stride=BY), :] = faces[c][3]


def parts_of(value):
    high = value.astype(jnp.bfloat16)
    return high, (value - high.astype(jnp.float32)).astype(jnp.bfloat16)


def pick_kernel(group, apart, info, flux, inner, velocity, *refs):
    arrived, (live, cells, base, weight) = refs[:4], refs[4:8]
    valve, payload, done, table, hits, next_hits, rows_even, rows_odd, sem = refs[8:]
    owners = cells.shape[0]
    add_faces(swept_faces(info, flux, 1, inner, velocity, None, arrived), inner, done)
    stored = [[pltpu.make_async_copy(done, valve, sem.at[0])]]
    each(stored, "start")
    for v in range(NVAR):
        across = done[v].T
        high, low = parts_of(across)
        table[v * BZ : (v + 1) * BZ, 0:PLANES] = high
        table[v * BZ : (v + 1) * BZ, PLANES : 2 * PLANES] = low
    plane_at = lax.broadcasted_iota(jnp.int32, (PLANES, CAP), 0)
    row_at = lax.broadcasted_iota(jnp.int32, (8, CAP), 0)
    unit = group + apart
    steps = owners // unit

    def find(index, target):
        for k in range(group):
            plane = lax.shift_right_logical(cells[pl.ds(index * unit + k, 1), :], 7)
            hit = jnp.where(plane_at == plane, 1.0, 0.0).astype(jnp.bfloat16)
            target[0:PLANES, k * CAP : (k + 1) * CAP] = hit
            target[PLANES:, k * CAP : (k + 1) * CAP] = hit

    def fetch(source, target):
        target[...] = jnp.dot(table[...], source[...], preferred_element_type=jnp.float32)

    def send(owner, found):
        keep = live[pl.ds(owner, 1), :] != 0.0
        parts = [weight[corner, pl.ds(owner, 1), :] for corner in range(7)]
        parts += [jnp.where(keep, jnp.sum(found[v], axis=0, keepdims=True), 0.0) for v in range(NVAR)]
        parts += [base[pl.ds(owner, 1), :].astype(jnp.float32)]
        for at, part in enumerate(parts):
            payload[owner, :, at * CAP : (at + 1) * CAP] = part

    def put(index, rows):
        for k in range(group):
            owner = index * unit + k
            depth = jnp.bitwise_and(cells[pl.ds(owner, 1), :], BZ - 1)
            offset = jnp.broadcast_to(depth, (8, CAP)) - row_at
            found = [jnp.zeros((8, CAP), jnp.float32)] * NVAR
            for z in range(0, BZ, 8):
                here = offset == z
                for v in range(NVAR):
                    row = rows[v * BZ + z : v * BZ + z + 8, k * CAP : (k + 1) * CAP]
                    found[v] = jnp.where(here, row, found[v])
            send(owner, found)

    def look_up(index):
        for k in range(apart):
            owner = index * unit + group + k
            cell = jnp.broadcast_to(cells[pl.ds(owner, 1), :], (8, CAP))
            depth = jnp.bitwise_and(cell, BZ - 1)
            offset = lax.shift_right_logical(cell, 7) - row_at
            found = [jnp.zeros((8, CAP), jnp.float32)] * NVAR
            for p in range(0, PLANES, 8):
                here = offset == p
                for v in range(NVAR):
                    row = jnp.take_along_axis(done[v, p : p + 8, :], depth, axis=1)
                    found[v] = jnp.where(here, row, found[v])
            send(owner, found)

    find(0, hits)
    fetch(hits, rows_even)
    look_up(0)
    find(1, next_hits)
    fetch(next_hits, rows_odd)
    put(0, rows_even)
    look_up(1)

    def step(pair, carry):
        one, two = 2 * pair, 2 * pair + 1
        find(one, hits)
        fetch(hits, rows_even)
        put(one - 1, rows_odd)
        look_up(one)
        find(two, next_hits)
        fetch(next_hits, rows_odd)
        put(one, rows_even)
        look_up(two)
        return carry

    lax.fori_loop(1, steps // 2, step, 0)
    put(steps - 1, rows_odd)
    each(stored, "wait")


def pick(info, flux, inner, velocity, arrived, live, cells, base, weight):
    owners = cells.shape[0]
    group, apart = (12, 4) if owners % (2 * (12 + 4)) == 0 else (1, 0)
    slots = group * CAP
    return pl.pallas_call(
        functools.partial(pick_kernel, group, apart),
        out_shape=[f32(NVAR, PLANES, BZ), f32(owners, 1, SEND_ROWS * CAP)],
        in_specs=[VMEM] * 12,
        out_specs=[HBM, VMEM],
        scratch_shapes=[
            pltpu.VMEM((NVAR, PLANES, BZ), jnp.float32),
            pltpu.VMEM((NVAR * BZ, 2 * PLANES), jnp.bfloat16),
            pltpu.VMEM((2 * PLANES, slots), jnp.bfloat16),
            pltpu.VMEM((2 * PLANES, slots), jnp.bfloat16),
            pltpu.VMEM((NVAR * BZ, slots), jnp.float32),
            pltpu.VMEM((NVAR * BZ, slots), jnp.float32),
            pltpu.SemaphoreType.DMA((1,)),
        ],
        compiler_params=params(20),
        name="pick",
    )(info, flux, inner, velocity, *arrived, live, cells, base, weight)


def scatter_kernel(group, info, flux, inner, velocity, blanking, *refs):
    arrived, received = refs[:4], refs[4]
    out, swept, total, across, spread, placed, next_spread, next_placed, sem = refs[5:]
    width = group * CAP
    steps = received.shape[0] // group
    tile = 16
    plane_at = lax.broadcasted_iota(jnp.int32, (PLANES // tile, tile, CAP), 0) * tile
    plane_at = plane_at + lax.broadcasted_iota(jnp.int32, (PLANES // tile, tile, CAP), 1)
    plane_at = plane_at.astype(jnp.float32).astype(jnp.bfloat16)
    run_at, y_at = plane_at[: RUNS // tile], plane_at[: BY // tile]
    zero = jnp.zeros((), jnp.bfloat16)

    def wide(row):
        return jnp.broadcast_to(row, (tile, CAP)).astype(jnp.bfloat16)[None]

    def wide_parts(row):
        high = row.astype(jnp.bfloat16).astype(jnp.float32)
        return wide(high), wide(row - high)

    def row(sender, at):
        return received[sender, :, at * CAP : (at + 1) * CAP]

    def build(index, spread, placed):
        for k in range(group):
            sender = index * group + k
            cols = [slice(part * width + k * CAP, part * width + (k + 1) * CAP) for part in range(2)]
            anchor = row(sender, 12).astype(jnp.int32)
            weights = [row(sender, corner) for corner in range(7)]
            weights.append(1.0 - sum(weights))
            depth = jnp.bitwise_and(anchor, BZ - 1)
            place = jnp.bitwise_and(depth, RUN - 1)
            row_y = jnp.bitwise_and(lax.shift_right_logical(anchor, 7), BY - 1)
            row_x = wide(lax.shift_right_logical(anchor, 12).astype(jnp.float32))
            at_y = [y_at == wide((row_y + j).astype(jnp.float32)) for j in range(2)]
            at_x = [row_x == jnp.full((), x, jnp.bfloat16) for x in range(-1, BX)]
            for spot in range(RUN + 1):
                along_y = []
                for i in range(2):
                    high = low = zero
                    for j in range(2):
                        weight = jnp.where(place == spot, weights[4 * i + 2 * j], 0.0)
                        weight = jnp.where(place == spot - 1, weights[4 * i + 2 * j + 1], weight)
                        high_row, low_row = wide_parts(weight)
                        high = jnp.where(at_y[j], high_row, high)
                        low = jnp.where(at_y[j], low_row, low)
                    along_y.append((low, high))
                for x in range(BX):
                    rows = slice(spot * PLANES + x * BY, spot * PLANES + (x + 1) * BY)
                    for part in range(2):
                        value = jnp.where(at_x[x], along_y[1][part], zero)
                        value = jnp.where(at_x[x + 1], along_y[0][part], value)
                        spread[rows, cols[part]] = value.reshape(BY, CAP)
            here = run_at == wide(jnp.right_shift(depth, RUN.bit_length() - 1).astype(jnp.float32))
            for v in range(NVAR):
                rows = slice(v * RUNS, (v + 1) * RUNS)
                high_row, low_row = wide_parts(row(sender, 7 + v))
                placed[rows, cols[0]] = jnp.where(here, high_row, zero).reshape(RUNS, CAP)
                placed[rows, cols[1]] = jnp.where(here, low_row, zero).reshape(RUNS, CAP)

    def add(spread, placed):
        dims = (((1,), (1,)), ((), ()))
        high_spread = spread[:, width:]
        product = lax.dot_general(placed[:, :width], spread[:, :width], dims, preferred_element_type=jnp.float32)
        values = jnp.concatenate([placed[:, :width], placed[:, width:]], axis=0)
        both = lax.dot_general(values, high_spread, dims, preferred_element_type=jnp.float32)
        product = product + (both[: NVAR * RUNS] + both[NVAR * RUNS :])
        total[...] += product

    total[...] = jnp.zeros_like(total)
    build(0, spread, placed)

    def step(pair, carry):
        add(spread, placed)
        build(2 * pair + 1, next_spread, next_placed)
        add(next_spread, next_placed)
        build(2 * pair + 2, spread, placed)
        return carry

    lax.fori_loop(0, steps // 2 - 1, step, 0)
    add(spread, placed)
    build(steps - 1, next_spread, next_placed)
    add_faces(swept_faces(info, flux, 0, inner, velocity, blanking, arrived), inner, swept)
    add(next_spread, next_placed)
    run = lax.broadcasted_iota(jnp.int32, (RUNS, PLANES), 0)
    stored = [[pltpu.make_async_copy(swept.at[v], out.at[v], sem.at[v])] for v in range(NVAR)]
    for v in range(NVAR):
        rows = slice(v * RUNS, (v + 1) * RUNS)
        for spot in range(RUN):
            block = total[rows, spot * PLANES : (spot + 1) * PLANES]
            if spot == 0:
                after = pltpu.roll(total[rows, RUN * PLANES :], 1, 0)
                block = block + jnp.where(run == 0, 0.0, after)
            for half in range(PLANES // CAP):
                cols = slice(half * CAP, (half + 1) * CAP)
                across[half, pl.ds(spot, RUNS, stride=RUN), :] = block[:, cols]
        for half in range(PLANES // CAP):
            planes = slice(half * CAP, (half + 1) * CAP)
            swept[v, planes, :] = swept[v, planes, :] + across[half].T
        each(stored[v : v + 1], "start")
    each(stored, "wait")


def scatter(info, flux, inner, velocity, blanking, arrived, received):
    senders = received.shape[0]
    group = 4 if senders % 8 == 0 else 1
    columns = 2 * group * CAP
    return pl.pallas_call(
        functools.partial(scatter_kernel, group),
        out_shape=f32(NVAR, PLANES, BZ),
        in_specs=[VMEM] * 10,
        out_specs=HBM,
        scratch_shapes=[
            pltpu.VMEM((NVAR, PLANES, BZ), jnp.float32),
            pltpu.VMEM((NVAR * RUNS, (RUN + 1) * PLANES), jnp.float32),
            pltpu.VMEM((PLANES // CAP, BZ, CAP), jnp.float32),
            pltpu.VMEM(((RUN + 1) * PLANES, columns), jnp.bfloat16),
            pltpu.VMEM((NVAR * RUNS, columns), jnp.bfloat16),
            pltpu.VMEM(((RUN + 1) * PLANES, columns), jnp.bfloat16),
            pltpu.VMEM((NVAR * RUNS, columns), jnp.bfloat16),
            pltpu.SemaphoreType.DMA((NVAR,)),
        ],
        compiler_params=params(32),
        name="scatter",
    )(info, flux, inner, velocity, blanking, *arrived, received)


def body(
    bulk,
    valve,
    bg_adjoint,
    bg_velocity,
    bg_source,
    bg_iblank,
    valve_adjoint,
    valve_velocity,
    valve_source,
    flux_mix,
    rec_cell,
    donor_base,
    donor_weight,
    slot_count,
):
    plans = face_plans(bulk, valve)
    info = flags(lax.axis_index("bulk"), bulk) + flags(lax.axis_index("valve"), valve)
    info = jnp.broadcast_to(jnp.stack(info).astype(jnp.int32)[:, None, None], (6, 8, BZ))
    flat = lambda block: block.reshape(-1, PLANES, BZ)
    bg, va = flat(bg_adjoint), flat(valve_adjoint)
    bg_fixed = (flat(bg_velocity), flat(bg_source), flat(bg_iblank))
    va_fixed = (flat(valve_velocity), flat(valve_source))
    *faces, bg, va = first_faces(info, bg, va)
    for repeat in range(ITERS):
        arrived = exchange(faces, plans)
        if repeat == 0:
            bg, va, bg_fixed, va_fixed, flux_wide, live = first_sweep(
                info, flux_mix, bg, va, bg_fixed, va_fixed, slot_count[:, None], faces
            )
        else:
            bg, va = sweep_inner(info, flux_wide, (bg, *bg_fixed), (va, *va_fixed), faces)
        if repeat < ITERS - 1:
            faces = next_faces(info, flux_wide, bg, bg_fixed[0], bg_fixed[2], va, va_fixed[0], arrived)
    va, payload = pick(
        info, flux_wide, va, va_fixed[0], arrived, live, rec_cell[0], donor_base[0], donor_weight[:, 0]
    )
    received = lax.all_to_all(payload, ("bulk", "valve"), split_axis=0, concat_axis=0, tiled=True)
    bg = scatter(info, flux_wide, bg, bg_fixed[0], bg_fixed[2], arrived, received)
    return (bg.reshape(bg_adjoint.shape), va.reshape(valve_adjoint.shape))


def solution(mesh):
    placed = (
        P(None, "bulk", "valve", None),
        P(None, "bulk", "valve", None),
        P(None, "bulk", "valve", None),
        P("bulk", "valve", None),
        P(None, "valve", "bulk", None),
        P(None, "valve", "bulk", None),
        P(None, "valve", "bulk", None),
        P(),
        P(("bulk", "valve"), None, None),
        P(("bulk", "valve"), None, None),
        P(None, ("bulk", "valve"), None, None),
        P(("bulk", "valve"), None),
    )
    return jax.shard_map(
        functools.partial(body, mesh.shape["bulk"], mesh.shape["valve"]),
        mesh=mesh,
        in_specs=placed,
        out_specs=(P(None, "bulk", "valve", None), P(None, "valve", "bulk", None)),
        check_vma=False,
    )
```

```python
import functools

import jax
import jax.numpy as jnp
from jax import lax
from jax.experimental import pallas as pl
from jax.experimental.pallas import tpu as pltpu
from jax.sharding import PartitionSpec as P

NVAR = 5
ITERS = 4
CAP = 128
BX = 8
BY = 32
BZ = 128
PLANES = BX * BY
FACE = BY + BX
STEP = BY + 16
SEND_ROWS = 13
RUN = 2
RUNS = BZ // RUN
PLACE = {(1, 0): 0, (1, 1): 1, (0, 1): 2, (0, 0): 3}

VMEM = pl.BlockSpec(memory_space=pltpu.VMEM)
SMEM = pl.BlockSpec(memory_space=pltpu.SMEM)
HBM = pl.BlockSpec(memory_space=pltpu.HBM)


def params(mib):
    return pltpu.CompilerParams(vmem_limit_bytes=mib * 1024 * 1024)


def in_hbm(x):
    return pltpu.with_memory_space_constraint(x, pltpu.HBM)


def f32(*shape):
    return jax.ShapeDtypeStruct(shape, jnp.float32)


def swap_pairs(count, odd):
    return {i: (i + 1 if i % 2 == odd else i - 1) % count for i in range(count)}


def face_plans(bulk, valve):
    number = lambda b, v: b * valve + v
    cells = [(b, v) for b in range(bulk) for v in range(valve)]
    plans = {}
    for odd in (0, 1):
        along_bulk, along_valve = swap_pairs(bulk, odd), swap_pairs(valve, odd)
        bulk_pairs, valve_pairs = [], []
        for b, v in cells:
            valve_end = odd and v in (0, valve - 1)
            bulk_pairs.append((number(b, v), number(along_bulk[b], v)))
            valve_pairs.append((number(b, v), number(b ^ 1, v) if valve_end else number(b, along_valve[v])))
        plans[0, odd], plans[1, odd] = bulk_pairs, valve_pairs
    return [plans[key] for key in sorted(PLACE, key=PLACE.get)]


def exchange(faces, plans):
    order = (2, 3, 0, 1)
    arrived = {k: lax.ppermute(faces[k], ("bulk", "valve"), plans[k]) for k in order}
    return [arrived[k] for k in range(4)]


def tall(tile, rows):
    return tile if rows == 8 else jnp.concatenate([tile] * (rows // 8), axis=0)


def flags(index, count):
    return [index % 2 == 0, index > 0, index < count - 1]


def flag(info, axis, which, rows):
    return tall(info[3 * axis + which], rows) != 0


def own_faces(info, axis_x, messages):
    faces = []
    for c in range(NVAR):
        sides = []
        for axis, start, size in ((axis_x, 0, BY), (1 - axis_x, BY, BX)):
            rows = slice(start, start + size)
            even, odd = messages[PLACE[axis, 0]][c, rows, :], messages[PLACE[axis, 1]][c, rows, :]
            is_even = flag(info, axis, 0, size)
            sides += [jnp.where(is_even, odd, even), jnp.where(is_even, even, odd)]
        faces.append(sides)
    return faces


def arrived_faces(info, axis_x, messages):
    faces = own_faces(info, axis_x, messages)
    for c in range(NVAR):
        for at, axis, size in ((0, axis_x, BY), (2, 1 - axis_x, BX)):
            for high in range(2):
                faces[c][at + high] = jnp.where(flag(info, axis, 1 + high, size), faces[c][at + high], 0.0)
    return faces


def send_faces(info, axis_x, faces, messages):
    for c in range(NVAR):
        for at, axis, start, size in ((0, axis_x, 0, BY), (2, 1 - axis_x, BY, BX)):
            rows = slice(start, start + size)
            low, high = faces[c][at : at + 2]
            is_even = flag(info, axis, 0, size)
            messages[PLACE[axis, 0]][c, rows, :] = jnp.where(is_even, high, low)
            messages[PLACE[axis, 1]][c, rows, :] = jnp.where(is_even, low, high)


def block_face(ref, c, side):
    if side == 0:
        return ref[c, 0:BY, :]
    if side == 1:
        return ref[c, PLANES - BY : PLANES, :]
    return ref[c, pl.ds(0 if side == 2 else BY - 1, BX, stride=BY), :]


def swept_faces(info, flux, axis_x, inner, velocity, blanking, messages):
    halos = arrived_faces(info, axis_x, messages)
    shares = []
    for side in range(4):
        d, sign = side // 2, 2.0 * (side % 2) - 1.0
        vel = [block_face(velocity, k, side) for k in range(3)]
        speed = 1.0 + (vel[0] * vel[0] + vel[1] * vel[1] + vel[2] * vel[2])
        slope = (0.5 * sign) * lax.rsqrt(speed) * vel[d]
        scale = 1.0 / 12.0
        if blanking is not None:
            scale = block_face(blanking, 0, side).astype(jnp.float32) * scale
        mixed = [slope * halos[j][side] for j in range(NVAR)]
        share = []
        for i in range(NVAR):
            total = halos[i][side]
            for j in range(NVAR):
                total = total + tall(flux[(d * NVAR + j) * NVAR + i], BY if d == 0 else BX) * mixed[j]
            share.append(scale * total)
        shares.append(share)
    x_row = lax.broadcasted_iota(jnp.int32, (BY, BZ), 0)
    y_row = lax.broadcasted_iota(jnp.int32, (BX, BZ), 0)
    faces = []
    for c in range(NVAR):
        xs = [block_face(inner, c, side) + shares[side][c] for side in range(2)]
        ys = [block_face(inner, c, side) + shares[side][c] for side in range(2, 4)]
        for k, at in enumerate((0, BX - 1)):
            for m, row in enumerate((0, BY - 1)):
                xs[k] = xs[k] + jnp.where(x_row == row, shares[2 + m][c][at : at + 1, :], 0.0)
                ys[m] = ys[m] + jnp.where(y_row == at, shares[k][c][row : row + 1, :], 0.0)
        faces.append(xs + ys)
    return faces


def loads(pairs, sem):
    copies = []
    for source, target in pairs:
        part = []
        for c in range(source.shape[0]):
            at = sum(map(len, copies)) + c
            part.append(pltpu.make_async_copy(source.at[c], target.at[c], sem.at[at]))
        copies.append(part)
    return copies


def each(copies, act):
    for part in copies:
        for copy in part:
            getattr(copy, act)()


def first_kernel(info, bg, va, *refs):
    messages, bg_here, va_here, sem = refs[:4], refs[4], refs[5], refs[6]
    copies = loads([(bg, bg_here), (va, va_here)], sem)
    each(copies, "start")
    for axis_x, grid in ((0, bg_here), (1, va_here)):
        each(copies[axis_x : axis_x + 1], "wait")
        faces = [[block_face(grid, c, side) for side in range(4)] for c in range(NVAR)]
        send_faces(info, axis_x, faces, messages)


def first_faces(info, bg, va):
    return pl.pallas_call(
        first_kernel,
        out_shape=[f32(NVAR, FACE, BZ)] * 4 + [f32(NVAR, PLANES, BZ)] * 2,
        in_specs=[VMEM, HBM, HBM],
        out_specs=[VMEM] * 6,
        scratch_shapes=[pltpu.SemaphoreType.DMA((2 * NVAR,))],
        compiler_params=params(4),
        name="first_faces",
    )(info, in_hbm(bg), in_hbm(va))


def faces_kernel(info, flux, bg, bg_velocity, blanking, va, va_velocity, *messages):
    arrived, sends = messages[:4], messages[4:]
    faces = swept_faces(info, flux, 0, bg, bg_velocity, blanking, arrived)
    send_faces(info, 0, faces, sends)
    faces = swept_faces(info, flux, 1, va, va_velocity, None, arrived)
    send_faces(info, 1, faces, sends)


def next_faces(info, flux, bg, bg_velocity, blanking, va, va_velocity, arrived):
    return pl.pallas_call(
        faces_kernel,
        out_shape=[f32(NVAR, FACE, BZ)] * 4,
        in_specs=[VMEM] * 11,
        out_specs=[VMEM] * 4,
        compiler_params=params(4),
        name="next_faces",
    )(info, flux, bg, bg_velocity, blanking, va, va_velocity, *arrived)


def fill_padded(faces, grid, padded):
    zeros = jnp.zeros((BY, BZ), jnp.float32)
    for c in range(NVAR):
        for x in range(-1, BX + 1):
            if x in (-1, BX):
                plane = zeros
            elif x in (0, BX - 1):
                plane = faces[c][0 if x == 0 else 1]
            else:
                plane = grid[c, x * BY : (x + 1) * BY, :]
            padded[c, (x + 1) * STEP + 8 : (x + 1) * STEP + 8 + BY, :] = plane
        for row, face in ((7, zeros[:BX]), (8, faces[c][2]), (7 + BY, faces[c][3]), (8 + BY, zeros[:BX])):
            padded[c, pl.ds(STEP + row, BX, stride=STEP), :] = face


def sweep(flux, padded, velocity, source, blanking, out):
    depth = lax.broadcasted_iota(jnp.int32, (BY, BZ), 1)
    first, last = depth == 0, depth == BZ - 1
    for x in range(BX):
        here = slice(x * BY, (x + 1) * BY)

        def near(j, dx, dy):
            start = (x + 1 + dx) * STEP + 8 + dy
            return padded[j, start : start + BY, :]

        vel = [velocity[d, here, :] for d in range(3)]
        speed = 1.0 + (vel[0] * vel[0] + vel[1] * vel[1] + vel[2] * vel[2])
        half = 0.5 * lax.rsqrt(speed)
        acc = [source[i, here, :] for i in range(NVAR)]
        for d in range(3):
            slope = half * vel[d]
            mixed = []
            for j in range(NVAR):
                if d == 0:
                    low, high = near(j, -1, 0), near(j, 1, 0)
                elif d == 1:
                    low, high = near(j, 0, -1), near(j, 0, 1)
                else:
                    mid = near(j, 0, 0)
                    low = jnp.where(first, 0.0, pltpu.roll(mid, 1, 1))
                    high = jnp.where(last, 0.0, pltpu.roll(mid, BZ - 1, 1))
                acc[j] = acc[j] + (low + high)
                mixed.append(slope * (high - low))
            for i in range(NVAR):
                for j in range(NVAR):
                    acc[i] = acc[i] + tall(flux[(d * NVAR + j) * NVAR + i], BY) * mixed[j]
        scale = 1.0 / 12.0
        if blanking is not None:
            scale = blanking[0, here, :].astype(jnp.float32) * scale
        for i in range(NVAR):
            out[i, here, :] = scale * acc[i]


def sweep_kernel(info, flux, *refs):
    bg, bg_velocity, bg_source, blanking, va, va_velocity, va_source = refs[:7]
    messages, (bg_out, va_out, bg_padded, va_padded) = refs[7:11], refs[11:]
    fill_padded(own_faces(info, 0, messages), bg, bg_padded)
    fill_padded(own_faces(info, 1, messages), va, va_padded)
    sweep(flux, bg_padded, bg_velocity, bg_source, blanking, bg_out)
    sweep(flux, va_padded, va_velocity, va_source, None, va_out)


def first_sweep_kernel(info, flux, bg, va, *refs):
    bg_velocity, blanking, va_velocity, sources, count = refs[0], refs[1], refs[2], refs[3:5], refs[5]
    messages, outs = refs[6:10], refs[10:]
    bg_out, va_out, here, wide, live = outs[0], outs[1], outs[2:4], outs[4], outs[5]
    bg_padded, va_padded, count_here, sem = outs[6:]
    copies = loads(list(zip(sources, here)) + [(count, count_here)], sem)
    each(copies, "start")
    fill_padded(own_faces(info, 0, messages), bg, bg_padded)
    fill_padded(own_faces(info, 1, messages), va, va_padded)
    each(copies[:1], "wait")
    for d in range(3):
        for j in range(NVAR):
            for i in range(NVAR):
                wide[(d * NVAR + j) * NVAR + i] = jnp.broadcast_to(flux[d, j : j + 1, i : i + 1], (8, BZ))
    sweep(wide, bg_padded, bg_velocity, here[0], blanking, bg_out)
    each(copies[1:], "wait")
    sweep(wide, va_padded, va_velocity, here[1], None, va_out)
    owners = count.shape[-1]
    counts = jnp.broadcast_to(count_here[0].astype(jnp.float32), (owners, owners))
    same = lax.broadcasted_iota(jnp.int32, (owners, owners), 0) == lax.broadcasted_iota(jnp.int32, (owners, owners), 1)
    counts = jnp.sum(jnp.where(same, counts, 0.0), axis=1, keepdims=True)
    slot_at = lax.broadcasted_iota(jnp.int32, (owners, CAP), 1).astype(jnp.float32)
    live[...] = jnp.where(slot_at < counts, 1.0, 0.0)


def sweep_cost():
    cells = BX * BY * BZ
    return pl.CostEstimate(flops=2 * cells * 230, bytes_accessed=4 * cells * 37, transcendentals=2 * cells)


def padded_scratch():
    return [pltpu.VMEM((NVAR, (BX + 2) * STEP, BZ), jnp.float32)] * 2


def first_sweep(info, flux, bg, va, bg_fixed, va_fixed, count, messages):
    sources = (bg_fixed[1], va_fixed[1])
    outs = pl.pallas_call(
        first_sweep_kernel,
        out_shape=[f32(NVAR, PLANES, BZ)] * 2 + [f32(NVAR, PLANES, BZ)] * 2
        + [f32(3 * NVAR * NVAR, 8, BZ), f32(count.shape[-1], CAP)],
        in_specs=[VMEM] * 7 + [HBM] * 3 + [VMEM] * 4,
        out_specs=[VMEM] * 6,
        scratch_shapes=padded_scratch()
        + [pltpu.VMEM(count.shape, jnp.int32), pltpu.SemaphoreType.DMA((2 * NVAR + 1,))],
        compiler_params=params(8),
        cost_estimate=sweep_cost(),
        name="first_sweep",
    )(info, flux, bg, va, bg_fixed[0], bg_fixed[2], va_fixed[0], *map(in_hbm, (*sources, count)), *messages)
    return outs[0], outs[1], (bg_fixed[0], outs[2], bg_fixed[2]), (va_fixed[0], outs[3]), outs[4], outs[5]


def sweep_inner(info, flux, bg, va, messages):
    return pl.pallas_call(
        sweep_kernel,
        out_shape=[f32(NVAR, PLANES, BZ)] * 2,
        in_specs=[VMEM] * 13,
        out_specs=[VMEM] * 2,
        scratch_shapes=padded_scratch(),
        compiler_params=params(8),
        cost_estimate=sweep_cost(),
        name="sweep_inner",
    )(info, flux, *bg, *va, *messages)


def add_faces(faces, inner, out):
    for c in range(NVAR):
        out[c, BY : PLANES - BY, :] = inner[c, BY : PLANES - BY, :]
        out[c, 0:BY, :] = faces[c][0]
        out[c, PLANES - BY : PLANES, :] = faces[c][1]
        out[c, pl.ds(0, BX, stride=BY), :] = faces[c][2]
        out[c, pl.ds(BY - 1, BX, stride=BY), :] = faces[c][3]


def parts_of(value):
    high = value.astype(jnp.bfloat16)
    return high, (value - high.astype(jnp.float32)).astype(jnp.bfloat16)


def pick_kernel(group, apart, info, flux, inner, velocity, *refs):
    arrived, (live, cells, base, weight) = refs[:4], refs[4:8]
    valve, payload, done, table, hits, next_hits, rows_even, rows_odd, sem = refs[8:]
    owners = cells.shape[0]
    add_faces(swept_faces(info, flux, 1, inner, velocity, None, arrived), inner, done)
    stored = [[pltpu.make_async_copy(done, valve, sem.at[0])]]
    each(stored, "start")
    for v in range(NVAR):
        across = done[v].T
        high, low = parts_of(across)
        table[v * BZ : (v + 1) * BZ, 0:PLANES] = high
        table[v * BZ : (v + 1) * BZ, PLANES : 2 * PLANES] = low
    plane_at = lax.broadcasted_iota(jnp.int32, (PLANES, CAP), 0)
    row_at = lax.broadcasted_iota(jnp.int32, (8, CAP), 0)
    unit = group + apart
    steps = owners // unit

    def find(index, target):
        for k in range(group):
            plane = lax.shift_right_logical(cells[pl.ds(index * unit + k, 1), :], 7)
            hit = jnp.where(plane_at == plane, 1.0, 0.0).astype(jnp.bfloat16)
            target[0:PLANES, k * CAP : (k + 1) * CAP] = hit
            target[PLANES:, k * CAP : (k + 1) * CAP] = hit

    def fetch(source, target):
        target[...] = jnp.dot(table[...], source[...], preferred_element_type=jnp.float32)

    def send(owner, found):
        keep = live[pl.ds(owner, 1), :] != 0.0
        parts = [weight[corner, pl.ds(owner, 1), :] for corner in range(7)]
        parts += [jnp.where(keep, jnp.sum(found[v], axis=0, keepdims=True), 0.0) for v in range(NVAR)]
        parts += [base[pl.ds(owner, 1), :].astype(jnp.float32)]
        for at, part in enumerate(parts):
            payload[owner, :, at * CAP : (at + 1) * CAP] = part

    def put(index, rows):
        for k in range(group):
            owner = index * unit + k
            depth = jnp.bitwise_and(cells[pl.ds(owner, 1), :], BZ - 1)
            offset = jnp.broadcast_to(depth, (8, CAP)) - row_at
            found = [jnp.zeros((8, CAP), jnp.float32)] * NVAR
            for z in range(0, BZ, 8):
                here = offset == z
                for v in range(NVAR):
                    row = rows[v * BZ + z : v * BZ + z + 8, k * CAP : (k + 1) * CAP]
                    found[v] = jnp.where(here, row, found[v])
            send(owner, found)

    def look_up(index):
        for k in range(apart):
            owner = index * unit + group + k
            cell = jnp.broadcast_to(cells[pl.ds(owner, 1), :], (8, CAP))
            depth = jnp.bitwise_and(cell, BZ - 1)
            offset = lax.shift_right_logical(cell, 7) - row_at
            found = [jnp.zeros((8, CAP), jnp.float32)] * NVAR
            for p in range(0, PLANES, 8):
                here = offset == p
                for v in range(NVAR):
                    row = jnp.take_along_axis(done[v, p : p + 8, :], depth, axis=1)
                    found[v] = jnp.where(here, row, found[v])
            send(owner, found)

    find(0, hits)
    fetch(hits, rows_even)
    look_up(0)
    find(1, next_hits)
    fetch(next_hits, rows_odd)
    put(0, rows_even)
    look_up(1)

    def step(pair, carry):
        one, two = 2 * pair, 2 * pair + 1
        find(one, hits)
        fetch(hits, rows_even)
        put(one - 1, rows_odd)
        look_up(one)
        find(two, next_hits)
        fetch(next_hits, rows_odd)
        put(one, rows_even)
        look_up(two)
        return carry

    lax.fori_loop(1, steps // 2, step, 0)
    put(steps - 1, rows_odd)
    each(stored, "wait")


def pick(info, flux, inner, velocity, arrived, live, cells, base, weight):
    owners = cells.shape[0]
    group, apart = (12, 4) if owners % (2 * (12 + 4)) == 0 else (1, 0)
    slots = group * CAP
    return pl.pallas_call(
        functools.partial(pick_kernel, group, apart),
        out_shape=[f32(NVAR, PLANES, BZ), f32(owners, 1, SEND_ROWS * CAP)],
        in_specs=[VMEM] * 12,
        out_specs=[HBM, VMEM],
        scratch_shapes=[
            pltpu.VMEM((NVAR, PLANES, BZ), jnp.float32),
            pltpu.VMEM((NVAR * BZ, 2 * PLANES), jnp.bfloat16),
            pltpu.VMEM((2 * PLANES, slots), jnp.bfloat16),
            pltpu.VMEM((2 * PLANES, slots), jnp.bfloat16),
            pltpu.VMEM((NVAR * BZ, slots), jnp.float32),
            pltpu.VMEM((NVAR * BZ, slots), jnp.float32),
            pltpu.SemaphoreType.DMA((1,)),
        ],
        compiler_params=params(20),
        name="pick",
    )(info, flux, inner, velocity, *arrived, live, cells, base, weight)


def scatter_kernel(group, info, flux, inner, velocity, blanking, *refs):
    arrived, received = refs[:4], refs[4]
    out, swept, total, across, spread, placed, next_spread, next_placed, sem = refs[5:]
    width = group * CAP
    steps = received.shape[0] // group
    tile = 16
    plane_at = lax.broadcasted_iota(jnp.int32, (PLANES // tile, tile, CAP), 0) * tile
    plane_at = plane_at + lax.broadcasted_iota(jnp.int32, (PLANES // tile, tile, CAP), 1)
    plane_at = plane_at.astype(jnp.float32).astype(jnp.bfloat16)
    run_at, y_at = plane_at[: RUNS // tile], plane_at[: BY // tile]
    zero = jnp.zeros((), jnp.bfloat16)

    def wide(row):
        return jnp.broadcast_to(row, (tile, CAP)).astype(jnp.bfloat16)[None]

    def wide_parts(row):
        high = row.astype(jnp.bfloat16).astype(jnp.float32)
        return wide(high), wide(row - high)

    def row(sender, at):
        return received[sender, :, at * CAP : (at + 1) * CAP]

    def build(index, spread, placed):
        for k in range(group):
            sender = index * group + k
            cols = [slice(part * width + k * CAP, part * width + (k + 1) * CAP) for part in range(2)]
            anchor = row(sender, 12).astype(jnp.int32)
            weights = [row(sender, corner) for corner in range(7)]
            weights.append(1.0 - sum(weights))
            depth = jnp.bitwise_and(anchor, BZ - 1)
            place = jnp.bitwise_and(depth, RUN - 1)
            row_y = jnp.bitwise_and(lax.shift_right_logical(anchor, 7), BY - 1)
            row_x = wide(lax.shift_right_logical(anchor, 12).astype(jnp.float32))
            at_y = [y_at == wide((row_y + j).astype(jnp.float32)) for j in range(2)]
            at_x = [row_x == jnp.full((), x, jnp.bfloat16) for x in range(-1, BX)]
            for spot in range(RUN + 1):
                along_y = []
                for i in range(2):
                    high = low = zero
                    for j in range(2):
                        weight = jnp.where(place == spot, weights[4 * i + 2 * j], 0.0)
                        weight = jnp.where(place == spot - 1, weights[4 * i + 2 * j + 1], weight)
                        high_row, low_row = wide_parts(weight)
                        high = jnp.where(at_y[j], high_row, high)
                        low = jnp.where(at_y[j], low_row, low)
                    along_y.append((low, high))
                for x in range(BX):
                    rows = slice(spot * PLANES + x * BY, spot * PLANES + (x + 1) * BY)
                    for part in range(2):
                        value = jnp.where(at_x[x], along_y[1][part], zero)
                        value = jnp.where(at_x[x + 1], along_y[0][part], value)
                        spread[rows, cols[part]] = value.reshape(BY, CAP)
            here = run_at == wide(jnp.right_shift(depth, RUN.bit_length() - 1).astype(jnp.float32))
            for v in range(NVAR):
                rows = slice(v * RUNS, (v + 1) * RUNS)
                high_row, low_row = wide_parts(row(sender, 7 + v))
                placed[rows, cols[0]] = jnp.where(here, high_row, zero).reshape(RUNS, CAP)
                placed[rows, cols[1]] = jnp.where(here, low_row, zero).reshape(RUNS, CAP)

    def add(spread, placed):
        dims = (((1,), (1,)), ((), ()))
        high_spread = spread[:, width:]
        product = lax.dot_general(placed[:, :width], spread[:, :width], dims, preferred_element_type=jnp.float32)
        values = jnp.concatenate([placed[:, :width], placed[:, width:]], axis=0)
        both = lax.dot_general(values, high_spread, dims, preferred_element_type=jnp.float32)
        product = product + (both[: NVAR * RUNS] + both[NVAR * RUNS :])
        total[...] += product

    total[...] = jnp.zeros_like(total)
    build(0, spread, placed)

    def step(pair, carry):
        add(spread, placed)
        build(2 * pair + 1, next_spread, next_placed)
        add(next_spread, next_placed)
        build(2 * pair + 2, spread, placed)
        return carry

    lax.fori_loop(0, steps // 2 - 1, step, 0)
    add(spread, placed)
    build(steps - 1, next_spread, next_placed)
    add_faces(swept_faces(info, flux, 0, inner, velocity, blanking, arrived), inner, swept)
    add(next_spread, next_placed)
    run = lax.broadcasted_iota(jnp.int32, (RUNS, PLANES), 0)
    stored = [[pltpu.make_async_copy(swept.at[v], out.at[v], sem.at[v])] for v in range(NVAR)]
    for v in range(NVAR):
        rows = slice(v * RUNS, (v + 1) * RUNS)
        for spot in range(RUN):
            block = total[rows, spot * PLANES : (spot + 1) * PLANES]
            if spot == 0:
                after = pltpu.roll(total[rows, RUN * PLANES :], 1, 0)
                block = block + jnp.where(run == 0, 0.0, after)
            for half in range(PLANES // CAP):
                cols = slice(half * CAP, (half + 1) * CAP)
                across[half, pl.ds(spot, RUNS, stride=RUN), :] = block[:, cols]
        for half in range(PLANES // CAP):
            planes = slice(half * CAP, (half + 1) * CAP)
            swept[v, planes, :] = swept[v, planes, :] + across[half].T
        each(stored[v : v + 1], "start")
    each(stored, "wait")


def scatter(info, flux, inner, velocity, blanking, arrived, received):
    senders = received.shape[0]
    group = 4 if senders % 8 == 0 else 1
    columns = 2 * group * CAP
    return pl.pallas_call(
        functools.partial(scatter_kernel, group),
        out_shape=f32(NVAR, PLANES, BZ),
        in_specs=[VMEM] * 10,
        out_specs=HBM,
        scratch_shapes=[
            pltpu.VMEM((NVAR, PLANES, BZ), jnp.float32),
            pltpu.VMEM((NVAR * RUNS, (RUN + 1) * PLANES), jnp.float32),
            pltpu.VMEM((PLANES // CAP, BZ, CAP), jnp.float32),
            pltpu.VMEM(((RUN + 1) * PLANES, columns), jnp.bfloat16),
            pltpu.VMEM((NVAR * RUNS, columns), jnp.bfloat16),
            pltpu.VMEM(((RUN + 1) * PLANES, columns), jnp.bfloat16),
            pltpu.VMEM((NVAR * RUNS, columns), jnp.bfloat16),
            pltpu.SemaphoreType.DMA((NVAR,)),
        ],
        compiler_params=params(32),
        name="scatter",
    )(info, flux, inner, velocity, blanking, *arrived, received)


def body(
    bulk,
    valve,
    bg_adjoint,
    bg_velocity,
    bg_source,
    bg_iblank,
    valve_adjoint,
    valve_velocity,
    valve_source,
    flux_mix,
    rec_cell,
    donor_base,
    donor_weight,
    slot_count,
):
    plans = face_plans(bulk, valve)
    info = flags(lax.axis_index("bulk"), bulk) + flags(lax.axis_index("valve"), valve)
    info = jnp.broadcast_to(jnp.stack(info).astype(jnp.int32)[:, None, None], (6, 8, BZ))
    flat = lambda block: block.reshape(-1, PLANES, BZ)
    bg, va = flat(bg_adjoint), flat(valve_adjoint)
    bg_fixed = (flat(bg_velocity), flat(bg_source), flat(bg_iblank))
    va_fixed = (flat(valve_velocity), flat(valve_source))
    *faces, bg, va = first_faces(info, bg, va)
    for repeat in range(ITERS):
        arrived = exchange(faces, plans)
        if repeat == 0:
            bg, va, bg_fixed, va_fixed, flux_wide, live = first_sweep(
                info, flux_mix, bg, va, bg_fixed, va_fixed, slot_count[:, None], faces
            )
        else:
            bg, va = sweep_inner(info, flux_wide, (bg, *bg_fixed), (va, *va_fixed), faces)
        if repeat < ITERS - 1:
            faces = next_faces(info, flux_wide, bg, bg_fixed[0], bg_fixed[2], va, va_fixed[0], arrived)
    va, payload = pick(
        info, flux_wide, va, va_fixed[0], arrived, live, rec_cell[0], donor_base[0], donor_weight[:, 0]
    )
    received = lax.all_to_all(payload, ("bulk", "valve"), split_axis=0, concat_axis=0, tiled=True)
    bg = scatter(info, flux_wide, bg, bg_fixed[0], bg_fixed[2], arrived, received)
    return (bg.reshape(bg_adjoint.shape), va.reshape(valve_adjoint.shape))


def solution(mesh):
    placed = (
        P(None, "bulk", "valve", None),
        P(None, "bulk", "valve", None),
        P(None, "bulk", "valve", None),
        P("bulk", "valve", None),
        P(None, "valve", "bulk", None),
        P(None, "valve", "bulk", None),
        P(None, "valve", "bulk", None),
        P(),
        P(("bulk", "valve"), None, None),
        P(("bulk", "valve"), None, None),
        P(None, ("bulk", "valve"), None, None),
        P(("bulk", "valve"), None),
    )
    return jax.shard_map(
        functools.partial(body, mesh.shape["bulk"], mesh.shape["valve"]),
        mesh=mesh,
        in_specs=placed,
        out_specs=(P(None, "bulk", "valve", None), P(None, "valve", "bulk", None)),
        check_vma=False,
    )
```
